32 devices in a mesh: lon: 2 (over y), lat: 4 (over z), depth: 4 (over x, core).
Axes of the slice: x: 2, y: 2, z: 4, core: 2. Of those that a mesh axis runs over, the one named last changes fastest.
Arguments:
- snapshots: float32 [32768, 256], P(('lon', 'lat', 'depth')), may hold values from -300 to 300
- live_rows: int32 [32], P(('lon', 'lat', 'depth')), may hold values from 128 to 1024, as said below
- column_order: int32 [256], replicated, may hold values from 0 to 255, each once
Outputs:
- snapshot_basis: float32 [32768, 256], P(('lon', 'lat', 'depth'))
- triangular: float32 [256, 256], replicated
- highpass: float32 [32768, 256], P(('lon', 'lat', 'depth'))
The draws below stay inside these ranges and needn't reach their ends.
Inputs may be any that keep to these rules, and one draw needn't show every extreme that they name: `live_rows`: each entry is a multiple of 128; some block has all 1024 rows live and some other block has 128.
All inputs are finite; a program needn't handle non-finite values.
Results may differ from the reference program's by a relative error of at most 0.00005.
Values sent between devices are 32-bit elements; how exact they have to be, the bound alone decides.
No kernel may reach another device: no remote copies, remote signals or barrier semaphores. Data moves between devices by JAX's collectives and lax.ppermute only.
A program may use at most 64 MiB of HBM per device.

```python
import jax
import jax.numpy as jnp
from jax import lax

S = 256
LOW = 32
ROWS_DEV = 1024
BLOCKS = 32
NROWS = 32768


def draw_snapshots(key, part):
    first = jax.random.fold_in(jax.random.fold_in(key, 11), 0)
    second = jax.random.fold_in(jax.random.fold_in(key, 11), 1)
    fourth = jax.random.fold_in(jax.random.fold_in(key, 11), 3)
    column_scale = jnp.exp(jax.random.uniform(first, (S,), jnp.float32, 0.0, 2.302585))
    block_index = (jnp.arange(NROWS, dtype=jnp.int32) // ROWS_DEV).astype(jnp.float32)
    ramp = block_index / (BLOCKS - 1)
    row_jitter = jax.random.uniform(fourth, (NROWS,), jnp.float32, 0.6, 1.4)
    values = jnp.clip(jax.random.normal(second, (NROWS, S), jnp.float32), -5.0, 5.0)
    row_scale = jnp.exp(ramp * 1.098612) * row_jitter
    result = values * column_scale[None, :] * row_scale[:, None]
    return jnp.clip(result, -300.0, 300.0).astype(jnp.float32)


def draw_live_rows(key, part):
    first, second, third = jax.random.split(jax.random.fold_in(key, 23), 3)
    counts = 128 * jax.random.randint(first, (BLOCKS,), 1, ROWS_DEV // 128 + 1)
    full_block = jax.random.randint(second, (), 0, BLOCKS)
    small_block = (full_block + 1 + jax.random.randint(third, (), 0, BLOCKS - 1)) % BLOCKS
    position = jnp.arange(BLOCKS, dtype=jnp.int32)
    counts = jnp.where(position == full_block, ROWS_DEV, counts)
    counts = jnp.where(position == small_block, 128, counts)
    return counts.astype(jnp.int32)


def setup_inputs(seed: int = 0) -> dict:
    seeds = jax.random.split(jax.random.key(seed), 4)
    return {
        "snapshots": draw_snapshots(jax.random.fold_in(seeds[3], 71), 0),
        "live_rows": draw_live_rows(jax.random.fold_in(seeds[3], 71), 0),
        "column_order": jax.random.permutation(seeds[2], S).astype(jnp.int32),
    }


def reference(snapshots, live_rows, column_order):
    picked = jnp.take(snapshots, column_order, axis=1)
    blocks = picked.reshape(-1, ROWS_DEV, S)
    live_mask = jnp.arange(ROWS_DEV, dtype=jnp.int32)[None, :] < live_rows[:, None]
    masked = jnp.where(live_mask[:, :, None], blocks, jnp.zeros_like(blocks)).reshape(-1, S)
    global_gram = lax.dot_general(masked, masked, (((0,), (0,)), ((), ())), precision=lax.Precision.HIGHEST) / NROWS
    lower_factor = jnp.linalg.cholesky(global_gram)
    triangular = lower_factor.T
    snapshot_basis = jax.scipy.linalg.solve_triangular(lower_factor, masked.T, lower=True).T
    highpass = masked - jnp.dot(snapshot_basis[:, :LOW], triangular[:LOW, :], precision=lax.Precision.HIGHEST)
    return (snapshot_basis, triangular, highpass)
```

```python
import functools

import jax
import jax.numpy as jnp
from jax import lax
from jax.experimental import pallas as pl
from jax.experimental.pallas import tpu as pltpu
from jax.sharding import PartitionSpec as P

LOW = 32
HALF = 128
TILE = 8
AXES = ("lon", "lat", "depth")
HIGHEST = lax.Precision.HIGHEST
VMEM_LIMIT = 48 * 1024 * 1024


def dot(a, b, dims=((1,), (0,))):
    return lax.dot_general(
        a, b, (dims, ((), ())), precision=HIGHEST, preferred_element_type=jnp.float32
    )


def one_hot(order_ref):
    count = order_ref.shape[1]
    source = lax.broadcasted_iota(jnp.int32, (count, count), 0)
    return jnp.where(source == order_ref[...], 1.0, 0.0).astype(jnp.float32)


def gram_kernel(live_ref, order_ref, x_ref, gram_ref, *, total_rows):
    rows = lax.broadcasted_iota(jnp.int32, x_ref.shape, 0)
    masked = jnp.where(rows < live_ref[0], x_ref[...], 0.0)
    gram = dot(masked, masked, ((0,), (0,))) / total_rows
    pick = one_hot(order_ref)
    gram_ref[...] = dot(pick, dot(gram, pick), ((0,), (0,)))


def sum_kernel(parts_ref, out_ref):
    total = jnp.sum(parts_ref[...], axis=0)
    out_ref[...] = jnp.broadcast_to(total[None], out_ref.shape)


def spread(value):
    return jnp.broadcast_to(value, (TILE, HALF))


def factor(matrix, upper_ref, inverse_ref, beside):
    steps = HALF // TILE
    lanes = lax.broadcasted_iota(jnp.int32, (TILE, HALF), 1)
    subs = lax.broadcasted_iota(jnp.int32, (TILE, HALF), 0)
    trail = [matrix[g * TILE : (g + 1) * TILE] for g in range(steps)]
    eye = [jnp.where(lanes == subs + g * TILE, 1.0, 0.0) for g in range(steps)]
    for s in range(steps):
        first = s * TILE
        column = [
            [spread(trail[g][:, first + m : first + m + 1]) for m in range(TILE)]
            for g in range(s, steps)
        ]
        d = [[spread(column[0][q][i : i + 1]) for q in range(i + 1)] for i in range(TILE)]
        r = [spread(trail[s][m : m + 1]) for m in range(TILE)]
        t = [spread(eye[s][m : m + 1]) for m in range(TILE)]
        ahead = list(column[1]) if s + 1 < steps else None
        inv = [None] * TILE
        for m in range(TILE):
            inv[m] = lax.rsqrt(d[m][m])
            for i in range(m + 1, TILE):
                d[i][m] = d[i][m] * inv[m]
            for q in range(m + 1, TILE):
                for i in range(q, TILE):
                    d[i][q] = d[i][q] - d[i][m] * d[q][m]
            r[m] = r[m] * inv[m]
            t[m] = t[m] * inv[m]
            for i in range(m + 1, TILE):
                r[i] = r[i] - d[i][m] * r[m]
                t[i] = t[i] - d[i][m] * t[m]
            if ahead is not None:
                ahead[m] = ahead[m] * inv[m]
                for q in range(m + 1, TILE):
                    ahead[q] = ahead[q] - d[q][m] * ahead[m]
        for m in range(TILE):
            upper_ref[first + m : first + m + 1, :] = r[m][0:1]
            inverse_ref[first + m : first + m + 1, :] = t[m][0:1]
        if ahead is not None:
            for m in range(TILE):
                trail[s + 1] = trail[s + 1] - ahead[m] * r[m]
                eye[s + 1] = eye[s + 1] - ahead[m] * t[m]
        if s + 2 < steps:
            zr, zt = list(r), list(t)
            for m in reversed(range(TILE)):
                zr[m] = zr[m] * inv[m]
                zt[m] = zt[m] * inv[m]
                for i in range(m):
                    zr[i] = zr[i] - d[m][i] * zr[m]
                    zt[i] = zt[i] - d[m][i] * zt[m]
            for g in range(s + 2, steps):
                for m in range(TILE):
                    trail[g] = trail[g] - column[g - s][m] * zr[m]
                    eye[g] = eye[g] - column[g - s][m] * zt[m]
        beside(s)


def finish_kernel(
    live_ref, order_ref, gram_ref, x_ref,
    basis_ref, tri_ref, high_ref,
    upper, inverse, picked, rest,
):
    rows = x_ref.shape[0]
    steps = HALF // TILE
    chunk = rows // steps
    pick = one_hot(order_ref)

    def pick_rows(s):
        at = slice(s * chunk, (s + 1) * chunk)
        row = lax.broadcasted_iota(jnp.int32, (chunk, x_ref.shape[1]), 0) + s * chunk
        picked[at] = dot(jnp.where(row < live_ref[0], x_ref[at], 0.0), pick)

    above = lax.broadcasted_iota(jnp.int32, (HALF, HALF), 0) <= lax.broadcasted_iota(
        jnp.int32, (HALF, HALF), 1
    )
    factor(gram_ref[:HALF, :HALF], upper, inverse, pick_rows)
    tri_ref[:HALF, :HALF] = jnp.where(above, upper[...], 0.0)
    tri_ref[HALF:, :HALF] = jnp.zeros((HALF, HALF), jnp.float32)
    first_inverse = inverse[...]
    corner = dot(first_inverse, gram_ref[:HALF, HALF:])
    tri_ref[:HALF, HALF:] = corner
    second = gram_ref[HALF:, HALF:] - dot(corner, corner, ((0,), (0,)))

    def first_half(s):
        at = slice(s * chunk, (s + 1) * chunk)
        left = dot(picked[at, :HALF], first_inverse, ((1,), (1,)))
        basis_ref[at, :HALF] = left
        rest[at] = picked[at, HALF:] - dot(left, corner)
        high_ref[at] = picked[at] - dot(left[:, :LOW], tri_ref[:LOW, :])

    factor(second, upper, inverse, first_half)
    tri_ref[HALF:, HALF:] = jnp.where(above, upper[...], 0.0)
    basis_ref[:, HALF:] = dot(rest[...], inverse[...], ((1,), (1,)))


def sum_over_devices(gram, devices):
    width = gram.shape[0]
    if width % (TILE * devices):
        return lax.psum(gram, AXES)
    parts = lax.all_to_all(gram.reshape(devices, width // devices, width), AXES, 0, 0)
    total = pl.pallas_call(
        sum_kernel, out_shape=jax.ShapeDtypeStruct(parts.shape, jnp.float32)
    )(parts)
    return lax.all_to_all(total, AXES, 0, 0).reshape(width, width)


def on_device(snapshots, live_rows, column_order, *, devices):
    rows, width = snapshots.shape
    smem = pl.BlockSpec(memory_space=pltpu.SMEM)
    vmem = pl.BlockSpec(memory_space=pltpu.VMEM)
    params = pltpu.CompilerParams(vmem_limit_bytes=VMEM_LIMIT)
    order = column_order.reshape(1, width)
    square = jax.ShapeDtypeStruct((width, width), jnp.float32)
    tall = jax.ShapeDtypeStruct((rows, width), jnp.float32)
    gram = pl.pallas_call(
        functools.partial(gram_kernel, total_rows=rows * devices),
        in_specs=[smem, vmem, vmem],
        out_specs=vmem,
        out_shape=square,
        compiler_params=params,
    )(live_rows, order, snapshots)
    gram = sum_over_devices(gram, devices)
    return pl.pallas_call(
        finish_kernel,
        in_specs=[smem, vmem, vmem, vmem],
        out_specs=[vmem, vmem, vmem],
        out_shape=[tall, square, tall],
        scratch_shapes=[
            pltpu.VMEM((HALF, HALF), jnp.float32),
            pltpu.VMEM((HALF, HALF), jnp.float32),
            pltpu.VMEM((rows, width), jnp.float32),
            pltpu.VMEM((rows, HALF), jnp.float32),
        ],
        compiler_params=params,
    )(live_rows, order, gram, snapshots)


def solution(mesh):
    placed = (P(AXES, None), P(AXES), P())
    return jax.shard_map(
        functools.partial(on_device, devices=mesh.size),
        mesh=mesh,
        in_specs=placed,
        out_specs=(P(AXES, None), P(), P(AXES, None)),
        check_vma=False,
    )
```

```python
import functools

import jax
import jax.numpy as jnp
from jax import lax
from jax.experimental import pallas as pl
from jax.experimental.pallas import tpu as pltpu
from jax.sharding import PartitionSpec as P

LOW = 32
HALF = 128
TILE = 8
WIDE = 2
AXES = ("lon", "lat", "depth")
HIGHEST = lax.Precision.HIGHEST
VMEM_LIMIT = 16 * 1024 * 1024
LOADS = 4
PIECES = 8


def dot(a, b, dims=((1,), (0,)), precision=None):
    return lax.dot_general(
        a, b, (dims, ((), ())), precision=precision, preferred_element_type=jnp.float32
    )


def halves(value):
    high = value.astype(jnp.bfloat16)
    return high, (value - high.astype(jnp.float32)).astype(jnp.bfloat16)


def one_hot(order_ref):
    count = order_ref.shape[1]
    source = lax.broadcasted_iota(jnp.int32, (count, count), 0)
    return jnp.where(source == order_ref[...], 1.0, 0.0).astype(jnp.bfloat16)


def square_iotas():
    return (
        lax.broadcasted_iota(jnp.int32, (HALF, HALF), 0),
        lax.broadcasted_iota(jnp.int32, (HALF, HALF), 1),
    )


def gram_kernel(live_ref, order_ref, x_ref, packed_ref, picked_ref, held, sems, *, total_rows):
    rows, width = held.shape
    chunk = rows // LOADS
    copies = []
    for c in range(LOADS):
        at = pl.ds(c * chunk, chunk)
        copies.append(pltpu.make_async_copy(x_ref.at[at], held.at[at], sems.at[c]))
        copies[-1].start()
    pick = one_hot(order_ref)
    both = jnp.zeros((width, width), jnp.float32)
    cross = jnp.zeros((width, width), jnp.float32)
    for c in range(LOADS):
        at = slice(c * chunk, (c + 1) * chunk)
        copies[c].wait()
        row = lax.broadcasted_iota(jnp.int32, (chunk, width), 0) + c * chunk
        x = jnp.where(row < live_ref[0], held[at], 0.0)
        high = x.astype(jnp.bfloat16)
        left = x - high.astype(jnp.float32)
        middle = left.astype(jnp.bfloat16)
        low = (left - middle.astype(jnp.float32)).astype(jnp.bfloat16)
        high, middle, low = dot(high, pick), dot(middle, pick), dot(low, pick)
        picked_ref[at] = high + (middle + low)
        high = high.astype(jnp.bfloat16)
        middle = middle.astype(jnp.bfloat16)
        low = low.astype(jnp.bfloat16)
        down = ((0,), (0,))
        both = both + (dot(high, high, down) + dot(middle, middle, down))
        cross = cross + (dot(high, middle, down) + dot(high, low, down))
    gram = (both + (cross + cross.T)) / total_rows
    i, j = square_iotas()
    packed_ref[:HALF] = gram[:HALF, HALF:]
    last = gram[HALF:, HALF:]
    packed_ref[HALF : 2 * HALF] = jnp.where(i <= j, gram[:HALF, :HALF], last)
    packed_ref[2 * HALF :] = jnp.zeros((packed_ref.shape[0] - 2 * HALF, HALF), jnp.float32)
    packed_ref[2 * HALF : 2 * HALF + 1] = jnp.sum(jnp.where(i == j, last, 0.0), 0, keepdims=True)


def sum_kernel(parts_ref, out_ref, *, devices):
    each = parts_ref.shape[0] // devices
    terms = [parts_ref[k * each : (k + 1) * each] for k in range(devices)]
    while len(terms) > 1:
        pairs = [a + b for a, b in zip(terms[::2], terms[1::2])]
        terms = pairs + terms[len(pairs) * 2 :]
    for k in range(devices):
        out_ref[k * each : (k + 1) * each] = terms[0]


def spread(value):
    return jnp.broadcast_to(value, (TILE, HALF))


def factor(matrix, upper_ref, inverse_ref, update_ref, beside):
    width = WIDE * TILE
    steps = HALF // width
    groups = HALF // TILE
    lanes = lax.broadcasted_iota(jnp.int32, (TILE, HALF), 1)
    subs = lax.broadcasted_iota(jnp.int32, (TILE, HALF), 0)
    rows = [matrix[g * TILE : (g + 1) * TILE] for g in range(groups)]
    update_ref[...] = jnp.zeros_like(update_ref)
    for s in range(steps):
        first = s * width
        mine = range(s * WIDE, (s + 1) * WIDE)
        near = range((s + 1) * WIDE, min((s + 2) * WIDE, groups))
        far = range((s + 2) * WIDE, groups)
        column = [[spread(rows[g][:, first + q : first + q + 1]) for g in mine] for q in range(width)]
        side = {
            g: [spread(rows[g][:, first + q : first + q + 1]) for q in range(width)] for g in near
        }
        panel = [rows[g] for g in mine]
        up, low, scale = [None] * WIDE, [None] * WIDE, [None] * WIDE
        for m in range(width):
            home, at = divmod(m, TILE)
            here = subs == at
            pivot = spread(column[m][home][at : at + 1])
            recip = 1.0 / pivot
            root = lax.rsqrt(pivot)
            times = list(column[m])
            times[home] = jnp.where(here, 0.0, times[home])
            times = [value * recip for value in times]
            for q in range(m + 1, width):
                value = spread(column[q][home][at : at + 1])
                column[q] = [c - t * value for c, t in zip(column[q], times)]
            row_up = spread(panel[home][at : at + 1]) * root
            lane = lanes == first + m
            panel = [
                jnp.where(lane, jnp.where(here, 1.0, 0.0) if h == home else 0.0, panel[h])
                for h in range(WIDE)
            ]
            row = spread(panel[home][at : at + 1])
            row_low = row * root
            if at:
                up[home] = jnp.where(here, row_up, up[home])
                low[home] = jnp.where(here, row_low, low[home])
                scale[home] = jnp.where(here, recip, scale[home])
            else:
                up[home], low[home], scale[home] = row_up, row_low, recip
            panel = [p - t * row for p, t in zip(panel, times)]
        for h, g in enumerate(mine):
            at = slice(g * TILE, (g + 1) * TILE)
            upper_ref[at] = jnp.where(lanes >= subs + g * TILE, up[h], 0.0)
            inverse_ref[at] = jnp.where(lanes <= subs + g * TILE, low[h], 0.0)
        inside = (lanes >= first) & (lanes < first + width)
        solved = [p * c for p, c in zip(panel, scale)]
        for g in near:
            terms = [
                side[g][h * TILE + i] * spread(solved[h][i : i + 1])
                for h in range(WIDE)
                for i in range(TILE)
            ]
            while len(terms) > 1:
                terms = [a + b for a, b in zip(terms[::2], terms[1::2])]
            rows[g] = jnp.where(inside, 0.0, rows[g]) - terms[0]
        if far:
            for h, g in enumerate(mine):
                update_ref[g * TILE : (g + 1) * TILE] = solved[h]
            if s:
                update_ref[first - width : first] = jnp.zeros((width, HALF), jnp.float32)
            change = dot(
                jnp.concatenate([rows[g] for g in far], 0), update_ref[...], precision=HIGHEST
            )
            for k, g in enumerate(far):
                rows[g] = jnp.where(inside, 0.0, rows[g]) - change[k * TILE : (k + 1) * TILE]
        beside(s)


def finish_kernel(
    packed_ref, picked_ref, basis_ref, tri_ref, high_ref,
    basis, tri, high, rest, upper, inverse, update, sems,
):
    rows = picked_ref.shape[0]
    chunk = rows // PIECES
    i, j = square_iotas()
    mixed = packed_ref[HALF : 2 * HALF]
    flipped = mixed.T
    first = jnp.where(i <= j, mixed, flipped)
    last = jnp.where(i > j, mixed, flipped)
    last = jnp.where(
        i == j, jnp.broadcast_to(packed_ref[2 * HALF : 2 * HALF + 1], (HALF, HALF)), last
    )
    side = packed_ref[:HALF]

    copies = []

    def send(source, target, at, lanes):
        copies.append(
            pltpu.make_async_copy(
                source.at[at, lanes], target.at[at, lanes], sems.at[len(copies)]
            )
        )
        copies[-1].start()

    left_lanes, right_lanes, all_lanes = pl.ds(0, HALF), pl.ds(HALF, HALF), pl.ds(0, 2 * HALF)
    factor(first, upper, inverse, update, lambda s: None)
    corner = dot(inverse[...], side, precision=HIGHEST)
    tri[:HALF, :HALF] = upper[...]
    tri[:HALF, HALF:] = corner
    tri[HALF:, :HALF] = jnp.zeros((HALF, HALF), jnp.float32)
    second = last - dot(corner, corner, ((0,), (0,)), HIGHEST)

    none = jnp.zeros((HALF, HALF), jnp.bfloat16)

    def inverse_weights():
        h, l = halves(inverse[...])
        return jnp.concatenate([jnp.concatenate([h, h], 1), jnp.concatenate([l, none], 1)], 0)

    def fold(value):
        return value[:, :HALF] + value[:, HALF:]

    to_left = inverse_weights()
    ch, cl = halves(corner)
    to_rest = jnp.concatenate([jnp.concatenate([ch, cl], 1), jnp.concatenate([ch, none], 1)], 0)
    th, tl = halves(tri[:LOW, :])
    blank = jnp.zeros((HALF - LOW, 2 * HALF), jnp.bfloat16)
    to_high = jnp.concatenate([th, blank, th, blank], 0)
    to_high_low = jnp.concatenate([tl, blank], 0)

    def first_half(s):
        at = slice(s * chunk, (s + 1) * chunk)
        xh, xl = halves(picked_ref[at, :HALF])
        left = fold(dot(jnp.concatenate([xh, xl], 1), to_left, ((1,), (1,))))
        basis[at, :HALF] = left
        lh, ll = halves(left)
        both = jnp.concatenate([lh, ll], 1)
        rest[at] = picked_ref[at, HALF:] - fold(dot(both, to_rest))
        high[at] = picked_ref[at] - (dot(both, to_high) + dot(lh, to_high_low))
        rows_at = pl.ds(s * chunk, chunk)
        send(basis, basis_ref, rows_at, left_lanes)
        send(high, high_ref, rows_at, all_lanes)

    factor(second, upper, inverse, update, first_half)
    tri[HALF:, HALF:] = upper[...]
    send(tri, tri_ref, pl.ds(0, 2 * HALF), all_lanes)
    to_right = inverse_weights()
    for s in range(PIECES):
        at = slice(s * chunk, (s + 1) * chunk)
        rh, rl = halves(rest[at])
        basis[at, HALF:] = fold(dot(jnp.concatenate([rh, rl], 1), to_right, ((1,), (1,))))
        send(basis, basis_ref, pl.ds(s * chunk, chunk), right_lanes)
    for copy in copies:
        copy.wait()


def sum_over_devices(packed, devices):
    if packed.shape[0] % devices:
        return lax.psum(packed, AXES)
    shape = packed.shape

    def exchange(value):
        value = value.reshape(shape[0], 1, shape[1])
        return lax.all_to_all(value, AXES, 0, 0, tiled=True).reshape(shape)

    total = pl.pallas_call(
        functools.partial(sum_kernel, devices=devices),
        in_specs=[pl.BlockSpec(memory_space=pltpu.VMEM)],
        out_specs=pl.BlockSpec(memory_space=pltpu.VMEM),
        out_shape=jax.ShapeDtypeStruct(shape, jnp.float32),
        compiler_params=pltpu.CompilerParams(vmem_limit_bytes=VMEM_LIMIT),
    )(exchange(packed))
    return exchange(total)


def on_device(snapshots, live_rows, column_order, *, devices):
    rows, width = snapshots.shape
    smem = pl.BlockSpec(memory_space=pltpu.SMEM)
    vmem = pl.BlockSpec(memory_space=pltpu.VMEM)
    hbm = pl.BlockSpec(memory_space=pl.ANY)
    params = pltpu.CompilerParams(vmem_limit_bytes=VMEM_LIMIT)
    square = jax.ShapeDtypeStruct((width, width), jnp.float32)
    tall = jax.ShapeDtypeStruct((rows, width), jnp.float32)
    packed_rows = width + 32
    packed, picked = pl.pallas_call(
        functools.partial(gram_kernel, total_rows=rows * devices),
        in_specs=[smem, vmem, hbm],
        out_specs=[vmem, vmem],
        out_shape=[jax.ShapeDtypeStruct((packed_rows, HALF), jnp.float32), tall],
        scratch_shapes=[
            pltpu.VMEM((rows, width), jnp.float32),
            pltpu.SemaphoreType.DMA((LOADS,)),
        ],
        compiler_params=params,
    )(live_rows, column_order.reshape(1, width), snapshots)
    packed = sum_over_devices(packed, devices)
    block = pltpu.VMEM((HALF, HALF), jnp.float32)
    return pl.pallas_call(
        finish_kernel,
        in_specs=[vmem, vmem],
        out_specs=[hbm, hbm, hbm],
        out_shape=[tall, square, tall],
        scratch_shapes=[
            pltpu.VMEM((rows, width), jnp.float32),
            pltpu.VMEM((width, width), jnp.float32),
            pltpu.VMEM((rows, width), jnp.float32),
            pltpu.VMEM((rows, HALF), jnp.float32),
            block,
            block,
            block,
            pltpu.SemaphoreType.DMA((3 * PIECES + 1,)),
        ],
        compiler_params=params,
    )(packed, picked)


def solution(mesh):
    placed = (P(AXES, None), P(AXES), P())
    return jax.shard_map(
        functools.partial(on_device, devices=mesh.size),
        mesh=mesh,
        in_specs=placed,
        out_specs=(P(AXES, None), P(), P(AXES, None)),
        check_vma=False,
    )
```

```python
import functools

import jax
import jax.numpy as jnp
from jax import lax
from jax.experimental import pallas as pl
from jax.experimental.pallas import tpu as pltpu
from jax.sharding import PartitionSpec as P

LOW = 32
HALF = 128
TILE = 8
WIDE = 2
AXES = ("lon", "lat", "depth")
VMEM_LIMIT = 16 * 1024 * 1024
LOADS = 2
PIECES = 8


def dot(a, b, dims=((1,), (0,)), precision=None):
    return lax.dot_general(
        a, b, (dims, ((), ())), precision=precision, preferred_element_type=jnp.float32
    )


def halves(value):
    high = value.astype(jnp.bfloat16)
    return high, (value - high.astype(jnp.float32)).astype(jnp.bfloat16)


def one_hot(order_ref):
    count = order_ref.shape[1]
    source = lax.broadcasted_iota(jnp.int32, (count, count), 0)
    return jnp.where(source == order_ref[...], 1.0, 0.0).astype(jnp.bfloat16)


def square_iotas():
    return (
        lax.broadcasted_iota(jnp.int32, (HALF, HALF), 0),
        lax.broadcasted_iota(jnp.int32, (HALF, HALF), 1),
    )


def gram_kernel(
    live_ref, order_in, x_ref, packed_ref, picked_ref, held, order_ref, sems, *, total_rows
):
    rows, width = held.shape
    chunk = rows // LOADS
    fetch_order = pltpu.make_async_copy(order_in, order_ref, sems.at[LOADS])
    fetch_order.start()
    copies = []
    for c in range(LOADS):
        at = pl.ds(c * chunk, chunk)
        copies.append(pltpu.make_async_copy(x_ref.at[at], held.at[at], sems.at[c]))
        copies[-1].start()
    fetch_order.wait()
    pick = one_hot(order_ref)
    both = jnp.zeros((width, width), jnp.float32)
    cross = jnp.zeros((width, width), jnp.float32)
    for c in range(LOADS):
        at = slice(c * chunk, (c + 1) * chunk)
        copies[c].wait()
        row = lax.broadcasted_iota(jnp.int32, (chunk, width), 0) + c * chunk
        x = jnp.where(row < live_ref[0], held[at], 0.0)
        high, middle, low = (dot(part, pick) for part in thirds(x))
        picked_ref[at] = high + (middle + low)
        high = high.astype(jnp.bfloat16)
        middle = middle.astype(jnp.bfloat16)
        low = low.astype(jnp.bfloat16)
        down = ((0,), (0,))
        both = both + (dot(high, high, down) + dot(middle, middle, down))
        cross = cross + (dot(high, middle, down) + dot(high, low, down))
    gram = (both + (cross + cross.T)) / total_rows
    i, j = square_iotas()
    packed_ref[:HALF] = gram[:HALF, HALF:]
    last = gram[HALF:, HALF:]
    packed_ref[HALF : 2 * HALF] = jnp.where(i <= j, gram[:HALF, :HALF], last)
    packed_ref[2 * HALF :] = jnp.zeros((packed_ref.shape[0] - 2 * HALF, HALF), jnp.float32)
    packed_ref[2 * HALF : 2 * HALF + 1] = jnp.sum(jnp.where(i == j, last, 0.0), 0, keepdims=True)


def sum_kernel(parts_ref, out_ref, *, devices):
    each = parts_ref.shape[0] // devices
    terms = [parts_ref[k * each : (k + 1) * each] for k in range(devices)]
    while len(terms) > 1:
        pairs = [a + b for a, b in zip(terms[::2], terms[1::2])]
        terms = pairs + terms[len(pairs) * 2 :]
    for k in range(devices):
        out_ref[k * each : (k + 1) * each] = terms[0]


def spread(value):
    return jnp.broadcast_to(value, (TILE, HALF))


def thirds(value):
    high = value.astype(jnp.bfloat16)
    rest = value - high.astype(jnp.float32)
    middle = rest.astype(jnp.bfloat16)
    return high, middle, (rest - middle.astype(jnp.float32)).astype(jnp.bfloat16)


def full_dot(a, b):
    ah, am, al = thirds(a)
    bh, bm, bl = thirds(b)
    pair = jnp.concatenate([bh, bm], 1)
    first = dot(jnp.concatenate([ah, am], 1), jnp.concatenate([pair, pair], 0))
    second = dot(jnp.concatenate([ah, al], 1), jnp.concatenate([bl, bh], 0))
    return first[:, :HALF] + (first[:, HALF:] + second)


def factor(matrix, upper_ref, inverse_ref, update_ref, beside):
    width = WIDE * TILE
    steps = HALF // width
    groups = HALF // TILE
    lanes = lax.broadcasted_iota(jnp.int32, (TILE, HALF), 1)
    subs = lax.broadcasted_iota(jnp.int32, (TILE, HALF), 0)
    rows = [matrix[g * TILE : (g + 1) * TILE] for g in range(groups)]
    update_ref[...] = jnp.zeros_like(update_ref)
    for s in range(steps):
        first = s * width
        mine = range(s * WIDE, (s + 1) * WIDE)
        near = range((s + 1) * WIDE, min((s + 2) * WIDE, groups))
        far = range((s + 2) * WIDE, groups)


        def pulled(g, q):
            only = jnp.where(lanes == first + q, rows[g], 0.0)
            return spread(jnp.sum(only, axis=1, keepdims=True))

        column = [[pulled(g, q) for g in mine] for q in range(width)]
        side = {g: [pulled(g, q) for q in range(width)] for g in near}
        panel = [rows[g] for g in mine]
        up, low, scale = [None] * WIDE, [None] * WIDE, [None] * WIDE
        for m in range(width):
            home, at = divmod(m, TILE)
            here = subs == at
            pivot = spread(column[m][home][at : at + 1])
            recip = 1.0 / pivot
            root = lax.rsqrt(pivot)
            times = list(column[m])
            times[home] = jnp.where(here, 0.0, times[home])
            times = [value * recip for value in times]
            for q in range(m + 1, width):
                value = spread(column[q][home][at : at + 1])
                column[q] = [c - t * value for c, t in zip(column[q], times)]
            row_up = spread(panel[home][at : at + 1]) * root
            lane = lanes == first + m
            panel = [
                jnp.where(lane, jnp.where(here, 1.0, 0.0) if h == home else 0.0, panel[h])
                for h in range(WIDE)
            ]
            row = spread(panel[home][at : at + 1])
            row_low = row * root
            if at:
                up[home] = jnp.where(here, row_up, up[home])
                low[home] = jnp.where(here, row_low, low[home])
                scale[home] = jnp.where(here, recip, scale[home])
            else:
                up[home], low[home], scale[home] = row_up, row_low, recip
            panel = [p - t * row for p, t in zip(panel, times)]
        for h, g in enumerate(mine):
            at = slice(g * TILE, (g + 1) * TILE)
            upper_ref[at] = jnp.where(lanes >= subs + g * TILE, up[h], 0.0)
            inverse_ref[at] = jnp.where(lanes <= subs + g * TILE, low[h], 0.0)
        inside = (lanes >= first) & (lanes < first + width)
        solved = [p * c for p, c in zip(panel, scale)]
        for g in near:
            terms = [
                side[g][h * TILE + i] * spread(solved[h][i : i + 1])
                for h in range(WIDE)
                for i in range(TILE)
            ]
            while len(terms) > 1:
                terms = [a + b for a, b in zip(terms[::2], terms[1::2])]
            rows[g] = jnp.where(inside, 0.0, rows[g]) - terms[0]
        if far:
            for h, g in enumerate(mine):
                update_ref[g * TILE : (g + 1) * TILE] = solved[h]
            if s:
                update_ref[first - width : first] = jnp.zeros((width, HALF), jnp.float32)
            change = full_dot(jnp.concatenate([rows[g] for g in far], 0), update_ref[...])
            for k, g in enumerate(far):
                rows[g] = jnp.where(inside, 0.0, rows[g]) - change[k * TILE : (k + 1) * TILE]
        beside(s)


def finish_kernel(
    packed_ref, picked_ref, basis_ref, tri_ref, high_ref,
    basis, tri, high, rest, upper, inverse, update, sems,
):
    rows = picked_ref.shape[0]
    chunk = rows // PIECES
    i, j = square_iotas()
    mixed = packed_ref[HALF : 2 * HALF]
    flipped = mixed.T
    first = jnp.where(i <= j, mixed, flipped)
    last = jnp.where(i > j, mixed, flipped)
    last = jnp.where(
        i == j, jnp.broadcast_to(packed_ref[2 * HALF : 2 * HALF + 1], (HALF, HALF)), last
    )
    side = packed_ref[:HALF]

    copies = []

    def send(source, target, at, lanes):
        copies.append(
            pltpu.make_async_copy(
                source.at[at, lanes], target.at[at, lanes], sems.at[len(copies)]
            )
        )
        copies[-1].start()

    left_lanes, right_lanes, all_lanes = pl.ds(0, HALF), pl.ds(HALF, HALF), pl.ds(0, 2 * HALF)
    factor(first, upper, inverse, update, lambda s: None)
    corner = full_dot(inverse[...], side)
    tri[:HALF, :HALF] = upper[...]
    tri[:HALF, HALF:] = corner
    tri[HALF:, :HALF] = jnp.zeros((HALF, HALF), jnp.float32)
    second = last - full_dot(corner.T, corner)

    none = jnp.zeros((HALF, HALF), jnp.bfloat16)

    def inverse_weights():
        h, l = halves(inverse[...])
        return jnp.concatenate([jnp.concatenate([h, h], 1), jnp.concatenate([l, none], 1)], 0)

    def fold(value):
        return value[:, :HALF] + value[:, HALF:]

    to_left = inverse_weights()
    ch, cl = halves(corner)
    to_rest = jnp.concatenate([jnp.concatenate([ch, cl], 1), jnp.concatenate([ch, none], 1)], 0)
    th, tl = halves(tri[:LOW, :])
    blank = jnp.zeros((HALF - LOW, 2 * HALF), jnp.bfloat16)
    to_high = jnp.concatenate([th, blank, th, blank], 0)
    to_high_low = jnp.concatenate([tl, blank], 0)

    def first_half(s):
        at = slice(s * chunk, (s + 1) * chunk)
        xh, xl = halves(picked_ref[at, :HALF])
        left = fold(dot(jnp.concatenate([xh, xl], 1), to_left, ((1,), (1,))))
        basis[at, :HALF] = left
        lh, ll = halves(left)
        both = jnp.concatenate([lh, ll], 1)
        rest[at] = picked_ref[at, HALF:] - fold(dot(both, to_rest))
        high[at] = picked_ref[at] - (dot(both, to_high) + dot(lh, to_high_low))
        rows_at = pl.ds(s * chunk, chunk)
        send(basis, basis_ref, rows_at, left_lanes)
        send(high, high_ref, rows_at, all_lanes)

    factor(second, upper, inverse, update, first_half)
    tri[HALF:, HALF:] = upper[...]
    send(tri, tri_ref, pl.ds(0, 2 * HALF), all_lanes)
    to_right = inverse_weights()
    for s in range(PIECES):
        at = slice(s * chunk, (s + 1) * chunk)
        rh, rl = halves(rest[at])
        basis[at, HALF:] = fold(dot(jnp.concatenate([rh, rl], 1), to_right, ((1,), (1,))))
        send(basis, basis_ref, pl.ds(s * chunk, chunk), right_lanes)
    for copy in copies:
        copy.wait()


def sum_over_devices(packed, devices):
    if packed.shape[0] % devices:
        return lax.psum(packed, AXES)
    shape = packed.shape

    def exchange(value):
        value = value.reshape(shape[0], 1, shape[1])
        return lax.all_to_all(value, AXES, 0, 0, tiled=True).reshape(shape)

    total = pl.pallas_call(
        functools.partial(sum_kernel, devices=devices),
        in_specs=[pl.BlockSpec(memory_space=pltpu.VMEM)],
        out_specs=pl.BlockSpec(memory_space=pltpu.VMEM),
        out_shape=jax.ShapeDtypeStruct(shape, jnp.float32),
        compiler_params=pltpu.CompilerParams(vmem_limit_bytes=VMEM_LIMIT),
    )(exchange(packed))
    return exchange(total)


def in_hbm(array):
    return pltpu.with_memory_space_constraint(array, pltpu.HBM)


def on_device(snapshots, live_rows, column_order, *, devices):
    rows, width = snapshots.shape
    smem = pl.BlockSpec(memory_space=pltpu.SMEM)
    vmem = pl.BlockSpec(memory_space=pltpu.VMEM)
    hbm = pl.BlockSpec(memory_space=pl.ANY)
    params = pltpu.CompilerParams(vmem_limit_bytes=VMEM_LIMIT)
    square = jax.ShapeDtypeStruct((width, width), jnp.float32)
    tall = jax.ShapeDtypeStruct((rows, width), jnp.float32)
    packed_rows = width + 32
    packed, picked = pl.pallas_call(
        functools.partial(gram_kernel, total_rows=rows * devices),
        in_specs=[smem, hbm, hbm],
        out_specs=[vmem, vmem],
        out_shape=[jax.ShapeDtypeStruct((packed_rows, HALF), jnp.float32), tall],
        scratch_shapes=[
            pltpu.VMEM((rows, width), jnp.float32),
            pltpu.VMEM((1, width), jnp.int32),
            pltpu.SemaphoreType.DMA((LOADS + 1,)),
        ],
        compiler_params=params,
    )(live_rows, in_hbm(column_order.reshape(1, width)), in_hbm(snapshots))
    packed = sum_over_devices(packed, devices)
    block = pltpu.VMEM((HALF, HALF), jnp.float32)
    return pl.pallas_call(
        finish_kernel,
        in_specs=[vmem, vmem],
        out_specs=[hbm, hbm, hbm],
        out_shape=[tall, square, tall],
        scratch_shapes=[
            pltpu.VMEM((rows, width), jnp.float32),
            pltpu.VMEM((width, width), jnp.float32),
            pltpu.VMEM((rows, width), jnp.float32),
            pltpu.VMEM((rows, HALF), jnp.float32),
            block,
            block,
            block,
            pltpu.SemaphoreType.DMA((3 * PIECES + 1,)),
        ],
        compiler_params=params,
    )(packed, picked)


def solution(mesh):
    placed = (P(AXES, None), P(AXES), P())
    return jax.shard_map(
        functools.partial(on_device, devices=mesh.size),
        mesh=mesh,
        in_specs=placed,
        out_specs=(P(AXES, None), P(), P(AXES, None)),
        check_vma=False,
    )
```

```python
import functools
import itertools
import math

import jax
import jax.numpy as jnp
from jax import lax
from jax.experimental import pallas as pl
from jax.experimental.pallas import tpu as pltpu
from jax.sharding import PartitionSpec as P

LOW = 32
HALF = 128
TILE = 8
WIDE = 2
AXES = ("lon", "lat", "depth")
VMEM_LIMIT = 16 * 1024 * 1024
LOADS = 2
PIECES = 8


def dot(a, b, dims=((1,), (0,)), precision=None):
    return lax.dot_general(
        a, b, (dims, ((), ())), precision=precision, preferred_element_type=jnp.float32
    )


def halves(value):
    high = value.astype(jnp.bfloat16)
    return high, (value - high.astype(jnp.float32)).astype(jnp.bfloat16)


def one_hot(order_ref):
    count = order_ref.shape[1]
    source = lax.broadcasted_iota(jnp.int32, (count, count), 0)
    return jnp.where(source == order_ref[...], 1.0, 0.0).astype(jnp.bfloat16)


def square_iotas():
    return (
        lax.broadcasted_iota(jnp.int32, (HALF, HALF), 0),
        lax.broadcasted_iota(jnp.int32, (HALF, HALF), 1),
    )


def gram_kernel(
    live_ref, order_in, x_ref, packed_ref, picked_ref, held, order_ref, sems, *, total_rows
):
    rows, width = held.shape
    chunk = rows // LOADS
    fetch_order = pltpu.make_async_copy(order_in, order_ref, sems.at[LOADS])
    fetch_order.start()
    copies = []
    for c in range(LOADS):
        at = pl.ds(c * chunk, chunk)
        copies.append(pltpu.make_async_copy(x_ref.at[at], held.at[at], sems.at[c]))
        copies[-1].start()
    fetch_order.wait()
    pick = one_hot(order_ref)
    both = jnp.zeros((width, width), jnp.float32)
    cross = jnp.zeros((width, width), jnp.float32)
    for c in range(LOADS):
        at = slice(c * chunk, (c + 1) * chunk)
        copies[c].wait()
        row = lax.broadcasted_iota(jnp.int32, (chunk, width), 0) + c * chunk
        x = jnp.where(row < live_ref[0], held[at], 0.0)
        high, middle, low = (dot(part, pick) for part in thirds(x))
        picked_ref[at] = high + (middle + low)
        high = high.astype(jnp.bfloat16)
        middle = middle.astype(jnp.bfloat16)
        low = low.astype(jnp.bfloat16)
        down = ((0,), (0,))
        both = both + (dot(high, high, down) + dot(middle, middle, down))
        cross = cross + (dot(high, middle, down) + dot(high, low, down))
    gram = (both + (cross + cross.T)) / total_rows
    i, j = square_iotas()
    packed_ref[:HALF] = gram[:HALF, HALF:]
    last = gram[HALF:, HALF:]
    packed_ref[HALF : 2 * HALF] = jnp.where(i <= j, gram[:HALF, :HALF], last)
    packed_ref[2 * HALF :] = jnp.zeros((packed_ref.shape[0] - 2 * HALF, HALF), jnp.float32)
    packed_ref[2 * HALF : 2 * HALF + 1] = jnp.sum(jnp.where(i == j, last, 0.0), 0, keepdims=True)


def spread(value):
    return jnp.broadcast_to(value, (TILE, HALF))


def thirds(value):
    high = value.astype(jnp.bfloat16)
    rest = value - high.astype(jnp.float32)
    middle = rest.astype(jnp.bfloat16)
    return high, middle, (rest - middle.astype(jnp.float32)).astype(jnp.bfloat16)


def full_dot(a, b):
    ah, am, al = thirds(a)
    bh, bm, bl = thirds(b)
    pair = jnp.concatenate([bh, bm], 1)
    first = dot(jnp.concatenate([ah, am], 1), jnp.concatenate([pair, pair], 0))
    second = dot(jnp.concatenate([ah, al], 1), jnp.concatenate([bl, bh], 0))
    return first[:, :HALF] + (first[:, HALF:] + second)


def factor(matrix, upper_ref, inverse_ref, update_ref, beside):
    width = WIDE * TILE
    steps = HALF // width
    groups = HALF // TILE
    lanes = lax.broadcasted_iota(jnp.int32, (TILE, HALF), 1)
    subs = lax.broadcasted_iota(jnp.int32, (TILE, HALF), 0)
    rows = [matrix[g * TILE : (g + 1) * TILE] for g in range(groups)]
    update_ref[...] = jnp.zeros_like(update_ref)
    for s in range(steps):
        first = s * width
        mine = range(s * WIDE, (s + 1) * WIDE)
        near = range((s + 1) * WIDE, min((s + 2) * WIDE, groups))
        far = range((s + 2) * WIDE, groups)


        def pulled(g, q):
            only = jnp.where(lanes == first + q, rows[g], 0.0)
            return spread(jnp.sum(only, axis=1, keepdims=True))

        column = [[pulled(g, q) for g in mine] for q in range(width)]
        side = {g: [pulled(g, q) for q in range(width)] for g in near}
        panel = [rows[g] for g in mine]
        up, low, scale = [None] * WIDE, [None] * WIDE, [None] * WIDE
        for m in range(width):
            home, at = divmod(m, TILE)
            here = subs == at
            pivot = spread(column[m][home][at : at + 1])
            recip = 1.0 / pivot
            root = lax.rsqrt(pivot)
            times = list(column[m])
            times[home] = jnp.where(here, 0.0, times[home])
            times = [value * recip for value in times]
            for q in range(m + 1, width):
                value = spread(column[q][home][at : at + 1])
                column[q] = [c - t * value for c, t in zip(column[q], times)]
            row_up = spread(panel[home][at : at + 1]) * root
            lane = lanes == first + m
            panel = [
                jnp.where(lane, jnp.where(here, 1.0, 0.0) if h == home else 0.0, panel[h])
                for h in range(WIDE)
            ]
            row = spread(panel[home][at : at + 1])
            row_low = row * root
            if at:
                up[home] = jnp.where(here, row_up, up[home])
                low[home] = jnp.where(here, row_low, low[home])
                scale[home] = jnp.where(here, recip, scale[home])
            else:
                up[home], low[home], scale[home] = row_up, row_low, recip
            panel = [p - t * row for p, t in zip(panel, times)]
        for h, g in enumerate(mine):
            at = slice(g * TILE, (g + 1) * TILE)
            upper_ref[at] = jnp.where(lanes >= subs + g * TILE, up[h], 0.0)
            inverse_ref[at] = jnp.where(lanes <= subs + g * TILE, low[h], 0.0)
        inside = (lanes >= first) & (lanes < first + width)
        solved = [p * c for p, c in zip(panel, scale)]
        for g in near:
            terms = [
                side[g][h * TILE + i] * spread(solved[h][i : i + 1])
                for h in range(WIDE)
                for i in range(TILE)
            ]
            while len(terms) > 1:
                terms = [a + b for a, b in zip(terms[::2], terms[1::2])]
            rows[g] = jnp.where(inside, 0.0, rows[g]) - terms[0]
        if far:
            for h, g in enumerate(mine):
                update_ref[g * TILE : (g + 1) * TILE] = solved[h]
            if s:
                update_ref[first - width : first] = jnp.zeros((width, HALF), jnp.float32)
            change = full_dot(jnp.concatenate([rows[g] for g in far], 0), update_ref[...])
            for k, g in enumerate(far):
                rows[g] = jnp.where(inside, 0.0, rows[g]) - change[k * TILE : (k + 1) * TILE]
        beside(s)


def finish_kernel(
    packed_ref, picked_ref, basis_ref, tri_ref, high_ref,
    basis, tri, high, rest, upper, inverse, update, sems,
):
    rows = picked_ref.shape[0]
    chunk = rows // PIECES
    i, j = square_iotas()
    mixed = packed_ref[HALF : 2 * HALF]
    flipped = mixed.T
    first = jnp.where(i <= j, mixed, flipped)
    last = jnp.where(i > j, mixed, flipped)
    last = jnp.where(
        i == j, jnp.broadcast_to(packed_ref[2 * HALF : 2 * HALF + 1], (HALF, HALF)), last
    )
    side = packed_ref[:HALF]

    copies = []

    def send(source, target, at, lanes):
        copies.append(
            pltpu.make_async_copy(
                source.at[at, lanes], target.at[at, lanes], sems.at[len(copies)]
            )
        )
        copies[-1].start()

    left_lanes, right_lanes, all_lanes = pl.ds(0, HALF), pl.ds(HALF, HALF), pl.ds(0, 2 * HALF)
    factor(first, upper, inverse, update, lambda s: None)
    corner = full_dot(inverse[...], side)
    tri[:HALF, :HALF] = upper[...]
    tri[:HALF, HALF:] = corner
    tri[HALF:, :HALF] = jnp.zeros((HALF, HALF), jnp.float32)
    second = last - full_dot(corner.T, corner)

    none = jnp.zeros((HALF, HALF), jnp.bfloat16)

    def inverse_weights():
        h, l = halves(inverse[...])
        return jnp.concatenate([jnp.concatenate([h, h], 1), jnp.concatenate([l, none], 1)], 0)

    def fold(value):
        return value[:, :HALF] + value[:, HALF:]

    to_left = inverse_weights()
    ch, cl = halves(corner)
    to_rest = jnp.concatenate([jnp.concatenate([ch, cl], 1), jnp.concatenate([ch, none], 1)], 0)
    th, tl = halves(tri[:LOW, :])
    blank = jnp.zeros((HALF - LOW, 2 * HALF), jnp.bfloat16)
    to_high = jnp.concatenate([th, blank, th, blank], 0)
    to_high_low = jnp.concatenate([tl, blank], 0)

    def first_half(s):
        at = slice(s * chunk, (s + 1) * chunk)
        xh, xl = halves(picked_ref[at, :HALF])
        left = fold(dot(jnp.concatenate([xh, xl], 1), to_left, ((1,), (1,))))
        basis[at, :HALF] = left
        lh, ll = halves(left)
        both = jnp.concatenate([lh, ll], 1)
        rest[at] = picked_ref[at, HALF:] - fold(dot(both, to_rest))
        high[at] = picked_ref[at] - (dot(both, to_high) + dot(lh, to_high_low))
        rows_at = pl.ds(s * chunk, chunk)
        send(basis, basis_ref, rows_at, left_lanes)
        send(high, high_ref, rows_at, all_lanes)

    factor(second, upper, inverse, update, first_half)
    tri[HALF:, HALF:] = upper[...]
    send(tri, tri_ref, pl.ds(0, 2 * HALF), all_lanes)
    to_right = inverse_weights()
    for s in range(PIECES):
        at = slice(s * chunk, (s + 1) * chunk)
        rh, rl = halves(rest[at])
        basis[at, HALF:] = fold(dot(jnp.concatenate([rh, rl], 1), to_right, ((1,), (1,))))
        send(basis, basis_ref, pl.ds(s * chunk, chunk), right_lanes)
    for copy in copies:
        copy.wait()


def flipped(value, sizes, moves):
    axes = tuple(axis for axis, _ in moves)
    pairs = []
    for source in itertools.product(*(range(sizes[axis]) for axis in axes)):
        target = [place ^ bit for place, (_, bit) in zip(source, moves)]
        index = [0, 0]
        for axis, a, b in zip(axes, source, target):
            index = [index[0] * sizes[axis] + a, index[1] * sizes[axis] + b]
        pairs.append(tuple(index))
    return lax.ppermute(value, axes, pairs)


def sum_over_devices(packed, sizes):
    bits = [(axis, 1 << k) for axis in AXES for k in range(sizes[axis].bit_length() - 1)]
    if any(size & (size - 1) for size in sizes.values()) or len(bits) < 4:
        return lax.psum(packed, AXES)
    split = ("depth", 1)
    together = [("lon", 1), ("depth", 2)]
    bits = [bit for bit in bits if bit != split and bit not in together]
    half = packed.shape[0] // 2
    mine = lax.axis_index("depth") & 1
    parts = packed.reshape(2, half, packed.shape[1])
    total = lax.dynamic_index_in_dim(parts, mine, 0, False) + flipped(
        lax.dynamic_index_in_dim(parts, 1 - mine, 0, False), sizes, [split]
    )
    first = flipped(total, sizes, together[:1])
    second = flipped(total, sizes, together[1:])
    third = flipped(total, sizes, together)
    total = (total + first) + (second + third)
    for bit in bits:
        total = total + flipped(total, sizes, [bit])
    other = flipped(total, sizes, [split])
    top = jnp.where(mine == 0, total, other)
    return jnp.concatenate([top, jnp.where(mine == 0, other, total)], 0)


def in_hbm(array):
    return pltpu.with_memory_space_constraint(array, pltpu.HBM)


def on_device(snapshots, live_rows, column_order, *, sizes):
    rows, width = snapshots.shape
    smem = pl.BlockSpec(memory_space=pltpu.SMEM)
    vmem = pl.BlockSpec(memory_space=pltpu.VMEM)
    hbm = pl.BlockSpec(memory_space=pl.ANY)
    params = pltpu.CompilerParams(vmem_limit_bytes=VMEM_LIMIT)
    square = jax.ShapeDtypeStruct((width, width), jnp.float32)
    tall = jax.ShapeDtypeStruct((rows, width), jnp.float32)
    packed_rows = width + 2 * TILE
    packed, picked = pl.pallas_call(
        functools.partial(gram_kernel, total_rows=rows * math.prod(sizes.values())),
        in_specs=[smem, hbm, hbm],
        out_specs=[vmem, vmem],
        out_shape=[jax.ShapeDtypeStruct((packed_rows, HALF), jnp.float32), tall],
        scratch_shapes=[
            pltpu.VMEM((rows, width), jnp.float32),
            pltpu.VMEM((1, width), jnp.int32),
            pltpu.SemaphoreType.DMA((LOADS + 1,)),
        ],
        compiler_params=params,
    )(live_rows, in_hbm(column_order.reshape(1, width)), in_hbm(snapshots))
    packed = sum_over_devices(packed, sizes)
    block = pltpu.VMEM((HALF, HALF), jnp.float32)
    return pl.pallas_call(
        finish_kernel,
        in_specs=[vmem, vmem],
        out_specs=[hbm, hbm, hbm],
        out_shape=[tall, square, tall],
        scratch_shapes=[
            pltpu.VMEM((rows, width), jnp.float32),
            pltpu.VMEM((width, width), jnp.float32),
            pltpu.VMEM((rows, width), jnp.float32),
            pltpu.VMEM((rows, HALF), jnp.float32),
            block,
            block,
            block,
            pltpu.SemaphoreType.DMA((3 * PIECES + 1,)),
        ],
        compiler_params=params,
    )(packed, picked)


def solution(mesh):
    placed = (P(AXES, None), P(AXES), P())
    return jax.shard_map(
        functools.partial(on_device, sizes={axis: mesh.shape[axis] for axis in AXES}),
        mesh=mesh,
        in_specs=placed,
        out_specs=(P(AXES, None), P(), P(AXES, None)),
        check_vma=False,
    )
```

```python
import functools

import jax
import jax.numpy as jnp
from jax import lax
from jax.experimental import pallas as pl
from jax.experimental.pallas import tpu as pltpu
from jax.sharding import PartitionSpec as P

LOW = 32
HALF = 128
TILE = 8
WIDE = 2
AXES = ("lon", "lat", "depth")
VMEM_LIMIT = 16 * 1024 * 1024
LOADS = 2
PIECES = 8
LAST = 4


def dot(a, b, dims=((1,), (0,)), precision=None):
    return lax.dot_general(
        a, b, (dims, ((), ())), precision=precision, preferred_element_type=jnp.float32
    )


def halves(value):
    high = value.astype(jnp.bfloat16)
    return high, (value - high.astype(jnp.float32)).astype(jnp.bfloat16)


def one_hot(order_ref):
    count = order_ref.shape[1]
    source = lax.broadcasted_iota(jnp.int32, (count, count), 0)
    return jnp.where(source == order_ref[...], 1.0, 0.0).astype(jnp.bfloat16)


def square_iotas():
    return (
        lax.broadcasted_iota(jnp.int32, (HALF, HALF), 0),
        lax.broadcasted_iota(jnp.int32, (HALF, HALF), 1),
    )


def gram_kernel(
    live_ref, order_in, x_ref, packed_ref, picked_ref, held, order_ref, sems, *, total_rows
):
    rows, width = held.shape
    chunk = rows // LOADS
    fetch_order = pltpu.make_async_copy(order_in, order_ref, sems.at[LOADS])
    fetch_order.start()
    copies = []
    for c in range(LOADS):
        at = pl.ds(c * chunk, chunk)
        copies.append(pltpu.make_async_copy(x_ref.at[at], held.at[at], sems.at[c]))
        copies[-1].start()
    fetch_order.wait()
    pick = one_hot(order_ref)
    both = jnp.zeros((width, width), jnp.float32)
    cross = jnp.zeros((width, width), jnp.float32)
    for c in range(LOADS):
        at = slice(c * chunk, (c + 1) * chunk)
        copies[c].wait()
        row = lax.broadcasted_iota(jnp.int32, (chunk, width), 0) + c * chunk
        x = jnp.where(row < live_ref[0], held[at], 0.0)
        high, middle, low = (dot(part, pick) for part in thirds(x))
        picked_ref[at] = high + (middle + low)
        high = high.astype(jnp.bfloat16)
        middle = middle.astype(jnp.bfloat16)
        low = low.astype(jnp.bfloat16)
        down = ((0,), (0,))
        both = both + (dot(high, high, down) + dot(middle, middle, down))
        cross = cross + (dot(high, middle, down) + dot(high, low, down))
    gram = (both + (cross + cross.T)) / total_rows
    i, j = square_iotas()
    packed_ref[:HALF] = gram[:HALF, HALF:]
    last = gram[HALF:, HALF:]
    packed_ref[HALF : 2 * HALF] = jnp.where(i <= j, gram[:HALF, :HALF], last)
    packed_ref[2 * HALF :] = jnp.zeros((packed_ref.shape[0] - 2 * HALF, HALF), jnp.float32)
    packed_ref[2 * HALF : 2 * HALF + 1] = jnp.sum(jnp.where(i == j, last, 0.0), 0, keepdims=True)


def spread(value):
    return jnp.broadcast_to(value, (TILE, HALF))


def thirds(value):
    high = value.astype(jnp.bfloat16)
    rest = value - high.astype(jnp.float32)
    middle = rest.astype(jnp.bfloat16)
    return high, middle, (rest - middle.astype(jnp.float32)).astype(jnp.bfloat16)


def full_dot(a, b):
    ah, am, al = thirds(a)
    bh, bm, bl = thirds(b)
    pair = jnp.concatenate([bh, bm], 1)
    first = dot(jnp.concatenate([ah, am], 1), jnp.concatenate([pair, pair], 0))
    second = dot(jnp.concatenate([ah, al], 1), jnp.concatenate([bl, bh], 0))
    return first[:, :HALF] + (first[:, HALF:] + second)


def factor(matrix, upper_ref, inverse_ref, update_ref, beside):
    width = WIDE * TILE
    steps = HALF // width
    groups = HALF // TILE
    lanes = lax.broadcasted_iota(jnp.int32, (TILE, HALF), 1)
    subs = lax.broadcasted_iota(jnp.int32, (TILE, HALF), 0)
    rows = [matrix[g * TILE : (g + 1) * TILE] for g in range(groups)]
    update_ref[...] = jnp.zeros_like(update_ref)
    for s in range(steps):
        first = s * width
        mine = range(s * WIDE, (s + 1) * WIDE)
        near = range((s + 1) * WIDE, min((s + 2) * WIDE, groups))
        far = range((s + 2) * WIDE, groups)


        def pulled(g, q):
            only = jnp.where(lanes == first + q, rows[g], 0.0)
            return spread(jnp.sum(only, axis=1, keepdims=True))

        column = [[pulled(g, q) for g in mine] for q in range(width)]
        side = {g: [pulled(g, q) for q in range(width)] for g in near}
        panel = [rows[g] for g in mine]
        up, low, scale = [None] * WIDE, [None] * WIDE, [None] * WIDE
        for m in range(width):
            home, at = divmod(m, TILE)
            here = subs == at
            recip = 1.0 / spread(column[m][home][at : at + 1])
            times = list(column[m])
            times[home] = jnp.where(here, 0.0, times[home])
            times = [value * recip for value in times]
            for q in range(m + 1, width):
                value = spread(column[q][home][at : at + 1])
                column[q] = [c - t * value for c, t in zip(column[q], times)]
            lane = lanes == first + m
            up[home] = jnp.where(here, panel[home], up[home]) if at else panel[home]
            panel = [
                jnp.where(lane, jnp.where(here, 1.0, 0.0) if h == home else 0.0, panel[h])
                for h in range(WIDE)
            ]
            low[home] = jnp.where(here, panel[home], low[home]) if at else panel[home]
            scale[home] = jnp.where(here, recip, scale[home]) if at else recip
            row = spread(panel[home][at : at + 1])
            panel = [p - t * row for p, t in zip(panel, times)]
        for h, g in enumerate(mine):
            at = slice(g * TILE, (g + 1) * TILE)
            root = scale[h] * lax.rsqrt(scale[h])
            upper_ref[at] = jnp.where(lanes >= subs + g * TILE, up[h] * root, 0.0)
            inverse_ref[at] = jnp.where(lanes <= subs + g * TILE, low[h] * root, 0.0)
        inside = (lanes >= first) & (lanes < first + width)
        solved = [p * c for p, c in zip(panel, scale)]
        for g in near:
            terms = [
                side[g][h * TILE + i] * spread(solved[h][i : i + 1])
                for h in range(WIDE)
                for i in range(TILE)
            ]
            while len(terms) > 1:
                terms = [a + b for a, b in zip(terms[::2], terms[1::2])]
            rows[g] = jnp.where(inside, 0.0, rows[g]) - terms[0]
        if far:
            for h, g in enumerate(mine):
                update_ref[g * TILE : (g + 1) * TILE] = solved[h]
            if s:
                update_ref[first - width : first] = jnp.zeros((width, HALF), jnp.float32)
            change = full_dot(jnp.concatenate([rows[g] for g in far], 0), update_ref[...])
            for k, g in enumerate(far):
                rows[g] = jnp.where(inside, 0.0, rows[g]) - change[k * TILE : (k + 1) * TILE]
        beside(s)


def finish_kernel(
    packed_ref, picked_ref, basis_ref, tri_ref, high_ref,
    basis, tri, high, rest, upper, inverse, update, sems,
):
    rows = picked_ref.shape[0]
    chunk = rows // PIECES
    i, j = square_iotas()
    mixed = packed_ref[HALF : 2 * HALF]
    flipped = mixed.T
    first = jnp.where(i <= j, mixed, flipped)
    last = jnp.where(i > j, mixed, flipped)
    last = jnp.where(
        i == j, jnp.broadcast_to(packed_ref[2 * HALF : 2 * HALF + 1], (HALF, HALF)), last
    )
    side = packed_ref[:HALF]

    copies = []

    def send(source, target, at, lanes):
        copies.append(
            pltpu.make_async_copy(
                source.at[at, lanes], target.at[at, lanes], sems.at[len(copies)]
            )
        )
        copies[-1].start()

    left_lanes, right_lanes, all_lanes = pl.ds(0, HALF), pl.ds(HALF, HALF), pl.ds(0, 2 * HALF)
    factor(first, upper, inverse, update, lambda s: None)
    corner = full_dot(inverse[...], side)
    tri[:HALF, :HALF] = upper[...]
    tri[:HALF, HALF:] = corner
    tri[HALF:, :HALF] = jnp.zeros((HALF, HALF), jnp.float32)
    second = last - full_dot(corner.T, corner)

    none = jnp.zeros((HALF, HALF), jnp.bfloat16)

    def inverse_weights():
        h, l = halves(inverse[...])
        return jnp.concatenate([jnp.concatenate([h, h], 1), jnp.concatenate([l, none], 1)], 0)

    def fold(value):
        return value[:, :HALF] + value[:, HALF:]

    to_left = inverse_weights()
    ch, cl = halves(corner)
    to_rest = jnp.concatenate([jnp.concatenate([ch, cl], 1), jnp.concatenate([ch, none], 1)], 0)
    th, tl = halves(tri[:LOW, :])
    blank = jnp.zeros((HALF - LOW, 2 * HALF), jnp.bfloat16)
    to_high = jnp.concatenate([th, blank, th, blank], 0)
    to_high_low = jnp.concatenate([tl, blank], 0)

    def first_half(s):
        at = slice(s * chunk, (s + 1) * chunk)
        xh, xl = halves(picked_ref[at, :HALF])
        left = fold(dot(jnp.concatenate([xh, xl], 1), to_left, ((1,), (1,))))
        basis[at, :HALF] = left
        lh, ll = halves(left)
        both = jnp.concatenate([lh, ll], 1)
        rest[at] = picked_ref[at, HALF:] - fold(dot(both, to_rest))
        high[at] = picked_ref[at] - (dot(both, to_high) + dot(lh, to_high_low))
        rows_at = pl.ds(s * chunk, chunk)
        send(basis, basis_ref, rows_at, left_lanes)
        send(high, high_ref, rows_at, all_lanes)

    factor(second, upper, inverse, update, first_half)
    tri[HALF:, HALF:] = upper[...]
    send(tri, tri_ref, pl.ds(0, 2 * HALF), all_lanes)
    to_right = inverse_weights()
    chunk = rows // LAST
    for s in range(LAST):
        at = slice(s * chunk, (s + 1) * chunk)
        rh, rl = halves(rest[at])
        basis[at, HALF:] = fold(dot(jnp.concatenate([rh, rl], 1), to_right, ((1,), (1,))))
        send(basis, basis_ref, pl.ds(s * chunk, chunk), right_lanes)
    for copy in copies:
        copy.wait()


def sum_over_devices(packed, devices):
    if devices & (devices - 1) or devices < 32:
        return lax.psum(packed, AXES)

    def flip(value, masks):
        pairs = [(i, i ^ masks[i & 1]) for i in range(devices)]
        return lax.ppermute(value, AXES, pairs)

    def add_four(value, one, two):
        both = tuple(a ^ b for a, b in zip(one, two))
        first, second, third = flip(value, one), flip(value, two), flip(value, both)
        return (value + first) + (second + third)

    half = packed.shape[0] // 2
    mine = lax.axis_index(AXES) & 1
    parts = packed.reshape(2, half, packed.shape[1])
    total = lax.dynamic_index_in_dim(parts, mine, 0, False) + flip(
        lax.dynamic_index_in_dim(parts, 1 - mine, 0, False), (1, 1)
    )
    total = add_four(total, (2, 16), (8, 4))
    total = add_four(total, (16, 2), (4, 8))
    for bit in range(5, devices.bit_length() - 1):
        total = total + flip(total, (1 << bit, 1 << bit))
    other = flip(total, (1, 1))
    top = jnp.where(mine == 0, total, other)
    return jnp.concatenate([top, jnp.where(mine == 0, other, total)], 0)


def in_hbm(array):
    return pltpu.with_memory_space_constraint(array, pltpu.HBM)


def on_device(snapshots, live_rows, column_order, *, devices):
    rows, width = snapshots.shape
    smem = pl.BlockSpec(memory_space=pltpu.SMEM)
    vmem = pl.BlockSpec(memory_space=pltpu.VMEM)
    hbm = pl.BlockSpec(memory_space=pl.ANY)
    params = pltpu.CompilerParams(vmem_limit_bytes=VMEM_LIMIT)
    square = jax.ShapeDtypeStruct((width, width), jnp.float32)
    tall = jax.ShapeDtypeStruct((rows, width), jnp.float32)
    packed_rows = width + 2 * TILE
    packed, picked = pl.pallas_call(
        functools.partial(gram_kernel, total_rows=rows * devices),
        in_specs=[smem, hbm, hbm],
        out_specs=[vmem, vmem],
        out_shape=[jax.ShapeDtypeStruct((packed_rows, HALF), jnp.float32), tall],
        scratch_shapes=[
            pltpu.VMEM((rows, width), jnp.float32),
            pltpu.VMEM((1, width), jnp.int32),
            pltpu.SemaphoreType.DMA((LOADS + 1,)),
        ],
        compiler_params=params,
    )(live_rows, in_hbm(column_order.reshape(1, width)), in_hbm(snapshots))
    packed = sum_over_devices(packed, devices)
    block = pltpu.VMEM((HALF, HALF), jnp.float32)
    return pl.pallas_call(
        finish_kernel,
        in_specs=[vmem, vmem],
        out_specs=[hbm, hbm, hbm],
        out_shape=[tall, square, tall],
        scratch_shapes=[
            pltpu.VMEM((rows, width), jnp.float32),
            pltpu.VMEM((width, width), jnp.float32),
            pltpu.VMEM((rows, width), jnp.float32),
            pltpu.VMEM((rows, HALF), jnp.float32),
            block,
            block,
            block,
            pltpu.SemaphoreType.DMA((2 * PIECES + LAST + 1,)),
        ],
        compiler_params=params,
    )(packed, picked)


def solution(mesh):
    placed = (P(AXES, None), P(AXES), P())
    return jax.shard_map(
        functools.partial(on_device, devices=mesh.size),
        mesh=mesh,
        in_specs=placed,
        out_specs=(P(AXES, None), P(), P(AXES, None)),
        check_vma=False,
    )
```

```python
import functools

import jax
import jax.numpy as jnp
from jax import lax
from jax.experimental import pallas as pl
from jax.experimental.pallas import tpu as pltpu
from jax.sharding import PartitionSpec as P

LOW = 32
HALF = 128
TILE = 8
WIDE = 2
AXES = ("lon", "lat", "depth")
VMEM_LIMIT = 16 * 1024 * 1024
LOADS = 1
PIECES = 8
LAST = 4


def dot(a, b, dims=((1,), (0,)), precision=None):
    return lax.dot_general(
        a, b, (dims, ((), ())), precision=precision, preferred_element_type=jnp.float32
    )


def halves(value):
    high = value.astype(jnp.bfloat16)
    return high, (value - high.astype(jnp.float32)).astype(jnp.bfloat16)


def one_hot(order_ref):
    count = order_ref.shape[1]
    source = lax.broadcasted_iota(jnp.int32, (count, count), 0)
    return jnp.where(source == order_ref[...], 1.0, 0.0).astype(jnp.bfloat16)


def square_iotas():
    return (
        lax.broadcasted_iota(jnp.int32, (HALF, HALF), 0),
        lax.broadcasted_iota(jnp.int32, (HALF, HALF), 1),
    )


def gram_kernel(
    live_ref, order_in, x_ref, packed_ref, high_ref, low_ref, held, order_ref, sems, *, total_rows
):
    rows, width = held.shape
    chunk = rows // LOADS
    fetch_order = pltpu.make_async_copy(order_in, order_ref, sems.at[LOADS])
    fetch_order.start()
    copies = []
    for c in range(LOADS):
        at = pl.ds(c * chunk, chunk)
        copies.append(pltpu.make_async_copy(x_ref.at[at], held.at[at], sems.at[c]))
        copies[-1].start()
    fetch_order.wait()
    pick = one_hot(order_ref)
    both = jnp.zeros((width, width), jnp.float32)
    cross = jnp.zeros((width, width), jnp.float32)
    down = ((0,), (0,))
    for c in range(LOADS):
        at = slice(c * chunk, (c + 1) * chunk)
        copies[c].wait()
        row = lax.broadcasted_iota(jnp.int32, (chunk, width), 0) + c * chunk
        high, low = halves(jnp.where(row < live_ref[0], held[at], 0.0))
        high = dot(high, pick).astype(jnp.bfloat16)
        low = dot(low, pick).astype(jnp.bfloat16)
        high_ref[at] = high
        low_ref[at] = low
        both = both + (dot(high, high, down) + dot(low, low, down))
        cross = cross + dot(high, low, down)
    gram = (both + (cross + cross.T)) / total_rows
    i, j = square_iotas()
    packed_ref[:HALF] = gram[:HALF, HALF:]
    last = gram[HALF:, HALF:]
    packed_ref[HALF : 2 * HALF] = jnp.where(i <= j, gram[:HALF, :HALF], last)
    packed_ref[2 * HALF :] = jnp.zeros((packed_ref.shape[0] - 2 * HALF, HALF), jnp.float32)
    packed_ref[2 * HALF : 2 * HALF + 1] = jnp.sum(jnp.where(i == j, last, 0.0), 0, keepdims=True)


def spread(value):
    return jnp.broadcast_to(value, (TILE, HALF))


def thirds(value):
    high = value.astype(jnp.bfloat16)
    rest = value - high.astype(jnp.float32)
    middle = rest.astype(jnp.bfloat16)
    return high, middle, (rest - middle.astype(jnp.float32)).astype(jnp.bfloat16)


def full_dot(a, b):
    ah, am, al = thirds(a)
    bh, bm, bl = thirds(b)
    pair = jnp.concatenate([bh, bm], 1)
    first = dot(jnp.concatenate([ah, am], 1), jnp.concatenate([pair, pair], 0))
    second = dot(jnp.concatenate([ah, al], 1), jnp.concatenate([bl, bh], 0))
    return first[:, :HALF] + (first[:, HALF:] + second)


def factor(matrix, upper_ref, inverse_ref, update_ref, beside):
    width = WIDE * TILE
    steps = HALF // width
    groups = HALF // TILE
    lanes = lax.broadcasted_iota(jnp.int32, (TILE, HALF), 1)
    subs = lax.broadcasted_iota(jnp.int32, (TILE, HALF), 0)
    rows = [matrix[g * TILE : (g + 1) * TILE] for g in range(groups)]
    update_ref[...] = jnp.zeros_like(update_ref)
    for s in range(steps):
        first = s * width
        mine = range(s * WIDE, (s + 1) * WIDE)
        near = range((s + 1) * WIDE, min((s + 2) * WIDE, groups))
        far = range((s + 2) * WIDE, groups)


        def pulled(g, q):
            only = jnp.where(lanes == first + q, rows[g], 0.0)
            return spread(jnp.sum(only, axis=1, keepdims=True))

        column = [[pulled(g, q) for g in mine] for q in range(width)]
        side = {g: [pulled(g, q) for q in range(width)] for g in near}
        panel = [rows[g] for g in mine]
        up, low, scale = [None] * WIDE, [None] * WIDE, [None] * WIDE
        for m in range(width):
            home, at = divmod(m, TILE)
            here = subs == at
            recip = 1.0 / spread(column[m][home][at : at + 1])
            times = list(column[m])
            times[home] = jnp.where(here, 0.0, times[home])
            times = [value * recip for value in times]
            for q in range(m + 1, width):
                value = spread(column[q][home][at : at + 1])
                column[q] = [c - t * value for c, t in zip(column[q], times)]
            lane = lanes == first + m
            up[home] = jnp.where(here, panel[home], up[home]) if at else panel[home]
            panel = [
                jnp.where(lane, jnp.where(here, 1.0, 0.0) if h == home else 0.0, panel[h])
                for h in range(WIDE)
            ]
            low[home] = jnp.where(here, panel[home], low[home]) if at else panel[home]
            scale[home] = jnp.where(here, recip, scale[home]) if at else recip
            row = spread(panel[home][at : at + 1])
            panel = [p - t * row for p, t in zip(panel, times)]
        for h, g in enumerate(mine):
            at = slice(g * TILE, (g + 1) * TILE)
            root = scale[h] * lax.rsqrt(scale[h])
            upper_ref[at] = jnp.where(lanes >= subs + g * TILE, up[h] * root, 0.0)
            inverse_ref[at] = jnp.where(lanes <= subs + g * TILE, low[h] * root, 0.0)
        inside = (lanes >= first) & (lanes < first + width)
        solved = [p * c for p, c in zip(panel, scale)]
        for g in near:
            terms = [
                side[g][h * TILE + i] * spread(solved[h][i : i + 1])
                for h in range(WIDE)
                for i in range(TILE)
            ]
            while len(terms) > 1:
                terms = [a + b for a, b in zip(terms[::2], terms[1::2])]
            rows[g] = jnp.where(inside, 0.0, rows[g]) - terms[0]
        if far:
            for h, g in enumerate(mine):
                update_ref[g * TILE : (g + 1) * TILE] = solved[h]
            if s:
                update_ref[first - width : first] = jnp.zeros((width, HALF), jnp.float32)
            change = full_dot(jnp.concatenate([rows[g] for g in far], 0), update_ref[...])
            for k, g in enumerate(far):
                rows[g] = jnp.where(inside, 0.0, rows[g]) - change[k * TILE : (k + 1) * TILE]
        beside(s)


def finish_kernel(
    packed_ref, xh_ref, xl_ref, basis_ref, tri_ref, high_ref,
    basis, tri, high, rest, upper, inverse, update, sems,
):
    rows = xh_ref.shape[0]
    chunk = rows // PIECES
    i, j = square_iotas()
    mixed = packed_ref[HALF : 2 * HALF]
    flipped = mixed.T
    first = jnp.where(i <= j, mixed, flipped)
    last = jnp.where(i > j, mixed, flipped)
    last = jnp.where(
        i == j, jnp.broadcast_to(packed_ref[2 * HALF : 2 * HALF + 1], (HALF, HALF)), last
    )
    side = packed_ref[:HALF]

    copies = []

    def send(source, target, at, lanes):
        copies.append(
            pltpu.make_async_copy(
                source.at[at, lanes], target.at[at, lanes], sems.at[len(copies)]
            )
        )
        copies[-1].start()

    left_lanes, right_lanes, all_lanes = pl.ds(0, HALF), pl.ds(HALF, HALF), pl.ds(0, 2 * HALF)
    factor(first, upper, inverse, update, lambda s: None)
    corner = full_dot(inverse[...], side)
    tri[:HALF, :HALF] = upper[...]
    tri[:HALF, HALF:] = corner
    tri[HALF:, :HALF] = jnp.zeros((HALF, HALF), jnp.float32)
    second = last - full_dot(corner.T, corner)

    none = jnp.zeros((HALF, HALF), jnp.bfloat16)

    def inverse_weights():
        h, l = halves(inverse[...])
        return jnp.concatenate([jnp.concatenate([h, h], 1), jnp.concatenate([l, none], 1)], 0)

    def fold(value):
        return value[:, :HALF] + value[:, HALF:]

    to_left = inverse_weights()
    ch, cl = halves(corner)
    to_rest = jnp.concatenate([jnp.concatenate([ch, cl], 1), jnp.concatenate([ch, none], 1)], 0)
    th, tl = halves(tri[:LOW, :])
    blank = jnp.zeros((HALF - LOW, 2 * HALF), jnp.bfloat16)
    to_high = jnp.concatenate([th, blank, th, blank], 0)
    to_high_low = jnp.concatenate([tl, blank], 0)

    def first_half(s):
        at = slice(s * chunk, (s + 1) * chunk)
        xh, xl = xh_ref[at], xl_ref[at]
        left = fold(dot(jnp.concatenate([xh[:, :HALF], xl[:, :HALF]], 1), to_left, ((1,), (1,))))
        x = xh.astype(jnp.float32) + xl.astype(jnp.float32)
        basis[at, :HALF] = left
        lh, ll = halves(left)
        both = jnp.concatenate([lh, ll], 1)
        rest[at] = x[:, HALF:] - fold(dot(both, to_rest))
        high[at] = x - (dot(both, to_high) + dot(lh, to_high_low))
        rows_at = pl.ds(s * chunk, chunk)
        send(basis, basis_ref, rows_at, left_lanes)
        send(high, high_ref, rows_at, all_lanes)

    factor(second, upper, inverse, update, first_half)
    tri[HALF:, HALF:] = upper[...]
    send(tri, tri_ref, pl.ds(0, 2 * HALF), all_lanes)
    to_right = inverse_weights()
    chunk = rows // LAST
    for s in range(LAST):
        at = slice(s * chunk, (s + 1) * chunk)
        rh, rl = halves(rest[at])
        basis[at, HALF:] = fold(dot(jnp.concatenate([rh, rl], 1), to_right, ((1,), (1,))))
        send(basis, basis_ref, pl.ds(s * chunk, chunk), right_lanes)
    for copy in copies:
        copy.wait()


def sum_over_devices(packed, devices):
    if devices & (devices - 1) or devices < 32:
        return lax.psum(packed, AXES)

    def flip(value, masks):
        pairs = [(i, i ^ masks[i & 1]) for i in range(devices)]
        return lax.ppermute(value, AXES, pairs)

    def add_four(value, one, two):
        both = tuple(a ^ b for a, b in zip(one, two))
        first, second, third = flip(value, one), flip(value, two), flip(value, both)
        return (value + first) + (second + third)

    half = packed.shape[0] // 2
    mine = lax.axis_index(AXES) & 1
    parts = packed.reshape(2, half, packed.shape[1])
    total = lax.dynamic_index_in_dim(parts, mine, 0, False) + flip(
        lax.dynamic_index_in_dim(parts, 1 - mine, 0, False), (1, 1)
    )
    total = add_four(total, (2, 16), (8, 4))
    total = add_four(total, (16, 2), (4, 8))
    for bit in range(5, devices.bit_length() - 1):
        total = total + flip(total, (1 << bit, 1 << bit))
    other = flip(total, (1, 1))
    top = jnp.where(mine == 0, total, other)
    return jnp.concatenate([top, jnp.where(mine == 0, other, total)], 0)


def in_hbm(array):
    return pltpu.with_memory_space_constraint(array, pltpu.HBM)


def on_device(snapshots, live_rows, column_order, *, devices):
    rows, width = snapshots.shape
    smem = pl.BlockSpec(memory_space=pltpu.SMEM)
    vmem = pl.BlockSpec(memory_space=pltpu.VMEM)
    hbm = pl.BlockSpec(memory_space=pl.ANY)
    params = pltpu.CompilerParams(vmem_limit_bytes=VMEM_LIMIT)
    square = jax.ShapeDtypeStruct((width, width), jnp.float32)
    tall = jax.ShapeDtypeStruct((rows, width), jnp.float32)
    part = jax.ShapeDtypeStruct((rows, width), jnp.bfloat16)
    packed_rows = width + 2 * TILE
    packed, xh, xl = pl.pallas_call(
        functools.partial(gram_kernel, total_rows=rows * devices),
        in_specs=[smem, hbm, hbm],
        out_specs=[vmem, vmem, vmem],
        out_shape=[jax.ShapeDtypeStruct((packed_rows, HALF), jnp.float32), part, part],
        scratch_shapes=[
            pltpu.VMEM((rows, width), jnp.float32),
            pltpu.VMEM((1, width), jnp.int32),
            pltpu.SemaphoreType.DMA((LOADS + 1,)),
        ],
        compiler_params=params,
    )(live_rows, in_hbm(column_order.reshape(1, width)), in_hbm(snapshots))
    packed = sum_over_devices(packed, devices)
    block = pltpu.VMEM((HALF, HALF), jnp.float32)
    return pl.pallas_call(
        finish_kernel,
        in_specs=[vmem, vmem, vmem],
        out_specs=[hbm, hbm, hbm],
        out_shape=[tall, square, tall],
        scratch_shapes=[
            pltpu.VMEM((rows, width), jnp.float32),
            pltpu.VMEM((width, width), jnp.float32),
            pltpu.VMEM((rows, width), jnp.float32),
            pltpu.VMEM((rows, HALF), jnp.float32),
            block,
            block,
            block,
            pltpu.SemaphoreType.DMA((2 * PIECES + LAST + 1,)),
        ],
        compiler_params=params,
    )(packed, xh, xl)


def solution(mesh):
    placed = (P(AXES, None), P(AXES), P())
    return jax.shard_map(
        functools.partial(on_device, devices=mesh.size),
        mesh=mesh,
        in_specs=placed,
        out_specs=(P(AXES, None), P(), P(AXES, None)),
        check_vma=False,
    )
```

```python
import functools

import jax
import jax.numpy as jnp
from jax import lax
from jax.experimental import pallas as pl
from jax.experimental.pallas import tpu as pltpu
from jax.sharding import PartitionSpec as P

LOW = 32
HALF = 128
TILE = 8
WIDE = 2
AXES = ("lon", "lat", "depth")
VMEM_LIMIT = 16 * 1024 * 1024
LOADS = 1
PIECES = 8
LAST = 4


def dot(a, b, dims=((1,), (0,)), precision=None):
    return lax.dot_general(
        a, b, (dims, ((), ())), precision=precision, preferred_element_type=jnp.float32
    )


def halves(value):
    high = value.astype(jnp.bfloat16)
    return high, (value - high.astype(jnp.float32)).astype(jnp.bfloat16)


def one_hot(order_ref):
    count = order_ref.shape[1]
    source = lax.broadcasted_iota(jnp.int32, (count, count), 0)
    return jnp.where(source == order_ref[...], 1.0, 0.0).astype(jnp.bfloat16)


def square_iotas():
    return (
        lax.broadcasted_iota(jnp.int32, (HALF, HALF), 0),
        lax.broadcasted_iota(jnp.int32, (HALF, HALF), 1),
    )


def gram_kernel(
    live_ref, order_in, x_ref, packed_ref, high_ref, low_ref, held, order_ref, sems, *, total_rows
):
    rows, width = held.shape
    chunk = rows // LOADS
    fetch_order = pltpu.make_async_copy(order_in, order_ref, sems.at[LOADS])
    fetch_order.start()
    copies = []
    for c in range(LOADS):
        at = pl.ds(c * chunk, chunk)
        copies.append(pltpu.make_async_copy(x_ref.at[at], held.at[at], sems.at[c]))
        copies[-1].start()
    fetch_order.wait()
    pick = one_hot(order_ref)
    both = jnp.zeros((width, width), jnp.float32)
    cross = jnp.zeros((width, width), jnp.float32)
    down = ((0,), (0,))
    for c in range(LOADS):
        at = slice(c * chunk, (c + 1) * chunk)
        copies[c].wait()
        row = lax.broadcasted_iota(jnp.int32, (chunk, width), 0) + c * chunk
        high, low = halves(jnp.where(row < live_ref[0], held[at], 0.0))
        high = dot(high, pick).astype(jnp.bfloat16)
        low = dot(low, pick).astype(jnp.bfloat16)
        high_ref[at] = high
        low_ref[at] = low
        both = both + (dot(high, high, down) + dot(low, low, down))
        cross = cross + dot(high, low, down)
    gram = (both + (cross + cross.T)) / total_rows
    i, j = square_iotas()
    packed_ref[:HALF] = gram[:HALF, HALF:]
    last = gram[HALF:, HALF:]
    packed_ref[HALF : 2 * HALF] = jnp.where(i <= j, gram[:HALF, :HALF], last)
    packed_ref[2 * HALF :] = jnp.zeros((packed_ref.shape[0] - 2 * HALF, HALF), jnp.float32)
    packed_ref[2 * HALF : 2 * HALF + 1] = jnp.sum(jnp.where(i == j, last, 0.0), 0, keepdims=True)


def spread(value):
    return jnp.broadcast_to(value, (TILE, HALF))


def thirds(value):
    high = value.astype(jnp.bfloat16)
    rest = value - high.astype(jnp.float32)
    middle = rest.astype(jnp.bfloat16)
    return high, middle, (rest - middle.astype(jnp.float32)).astype(jnp.bfloat16)


def full_dot(a, b):
    ah, am, al = thirds(a)
    bh, bm, bl = thirds(b)
    pair = jnp.concatenate([bh, bm], 1)
    first = dot(jnp.concatenate([ah, am], 1), jnp.concatenate([pair, pair], 0))
    second = dot(jnp.concatenate([ah, al], 1), jnp.concatenate([bl, bh], 0))
    return first[:, :HALF] + (first[:, HALF:] + second)


def factor(matrix, upper_ref, inverse_ref, update_ref, beside):
    width = WIDE * TILE
    steps = HALF // width
    groups = HALF // TILE
    lanes = lax.broadcasted_iota(jnp.int32, (TILE, HALF), 1)
    subs = lax.broadcasted_iota(jnp.int32, (TILE, HALF), 0)
    rows = [matrix[g * TILE : (g + 1) * TILE] for g in range(groups)]
    update_ref[...] = jnp.zeros_like(update_ref)
    for s in range(steps):
        first = s * width
        mine = range(s * WIDE, (s + 1) * WIDE)
        near = range((s + 1) * WIDE, min((s + 2) * WIDE, groups))
        far = range((s + 2) * WIDE, groups)


        def pulled(g, q):
            only = jnp.where(lanes == first + q, rows[g], 0.0)
            return spread(jnp.sum(only, axis=1, keepdims=True))

        column = [[pulled(g, q) for g in mine] for q in range(width)]
        side = {g: [pulled(g, q) for q in range(width)] for g in near}
        panel = [rows[g] for g in mine]
        up, low, scale = [None] * WIDE, [None] * WIDE, [None] * WIDE
        for m in range(width):
            home, at = divmod(m, TILE)
            here = subs == at
            recip = 1.0 / spread(column[m][home][at : at + 1])
            times = list(column[m])
            times[home] = jnp.where(here, 0.0, times[home])
            times = [value * recip for value in times]
            for q in range(m + 1, width):
                value = spread(column[q][home][at : at + 1])
                column[q] = [c - t * value for c, t in zip(column[q], times)]
            lane = lanes == first + m
            up[home] = jnp.where(here, panel[home], up[home]) if at else panel[home]
            panel = [
                jnp.where(lane, jnp.where(here, 1.0, 0.0) if h == home else 0.0, panel[h])
                for h in range(WIDE)
            ]
            low[home] = jnp.where(here, panel[home], low[home]) if at else panel[home]
            scale[home] = jnp.where(here, recip, scale[home]) if at else recip
            row = spread(panel[home][at : at + 1])
            panel = [p - t * row for p, t in zip(panel, times)]
        for h, g in enumerate(mine):
            at = slice(g * TILE, (g + 1) * TILE)
            root = scale[h] * lax.rsqrt(scale[h])
            upper_ref[at] = jnp.where(lanes >= subs + g * TILE, up[h] * root, 0.0)
            inverse_ref[at] = jnp.where(lanes <= subs + g * TILE, low[h] * root, 0.0)
        inside = (lanes >= first) & (lanes < first + width)
        solved = [p * c for p, c in zip(panel, scale)]
        for g in near:
            terms = [
                side[g][h * TILE + i] * spread(solved[h][i : i + 1])
                for h in range(WIDE)
                for i in range(TILE)
            ]
            while len(terms) > 1:
                terms = [a + b for a, b in zip(terms[::2], terms[1::2])]
            rows[g] = jnp.where(inside, 0.0, rows[g]) - terms[0]
        if far:
            for h, g in enumerate(mine):
                update_ref[g * TILE : (g + 1) * TILE] = solved[h]
            if s:
                update_ref[first - width : first] = jnp.zeros((width, HALF), jnp.float32)
            change = full_dot(jnp.concatenate([rows[g] for g in far], 0), update_ref[...])
            for k, g in enumerate(far):
                rows[g] = jnp.where(inside, 0.0, rows[g]) - change[k * TILE : (k + 1) * TILE]
        beside(s)


def finish_kernel(
    packed_ref, xh_ref, xl_ref, basis_ref, tri_ref, high_ref,
    basis, tri, high, rest, upper, inverse, update, sems,
):
    rows = xh_ref.shape[0]
    chunk = rows // PIECES
    i, j = square_iotas()
    mixed = packed_ref[HALF : 2 * HALF]
    flipped = mixed.T
    first = jnp.where(i <= j, mixed, flipped)
    last = jnp.where(i > j, mixed, flipped)
    last = jnp.where(
        i == j, jnp.broadcast_to(packed_ref[2 * HALF : 2 * HALF + 1], (HALF, HALF)), last
    )
    side = packed_ref[:HALF]

    copies = []

    def send(source, target, at, lanes):
        copies.append(
            pltpu.make_async_copy(
                source.at[at, lanes], target.at[at, lanes], sems.at[len(copies)]
            )
        )
        copies[-1].start()

    left_lanes, right_lanes, all_lanes = pl.ds(0, HALF), pl.ds(HALF, HALF), pl.ds(0, 2 * HALF)
    factor(first, upper, inverse, update, lambda s: None)
    corner = full_dot(inverse[...], side)
    missed = side - full_dot(upper[...].T, corner)
    corner = corner + full_dot(inverse[...], missed)
    tri[:HALF, :HALF] = upper[...]
    tri[:HALF, HALF:] = corner
    tri[HALF:, :HALF] = jnp.zeros((HALF, HALF), jnp.float32)
    second = last - full_dot(corner.T, corner)

    none = jnp.zeros((HALF, HALF), jnp.bfloat16)

    def inverse_weights():
        h, l = halves(inverse[...])
        return jnp.concatenate([jnp.concatenate([h, h], 1), jnp.concatenate([l, none], 1)], 0)

    def fold(value):
        return value[:, :HALF] + value[:, HALF:]

    to_left = inverse_weights()
    ch, cl = halves(corner)
    to_rest = jnp.concatenate([jnp.concatenate([ch, cl], 1), jnp.concatenate([ch, none], 1)], 0)
    th, tl = halves(tri[:LOW, :])
    blank = jnp.zeros((HALF - LOW, 2 * HALF), jnp.bfloat16)
    to_high = jnp.concatenate([th, blank, th, blank], 0)
    to_high_low = jnp.concatenate([tl, blank], 0)

    def first_half(s):
        at = slice(s * chunk, (s + 1) * chunk)
        xh, xl = xh_ref[at], xl_ref[at]
        left = fold(dot(jnp.concatenate([xh[:, :HALF], xl[:, :HALF]], 1), to_left, ((1,), (1,))))
        x = xh.astype(jnp.float32) + xl.astype(jnp.float32)
        basis[at, :HALF] = left
        lh, ll = halves(left)
        both = jnp.concatenate([lh, ll], 1)
        rest[at] = x[:, HALF:] - fold(dot(both, to_rest))
        high[at] = x - (dot(both, to_high) + dot(lh, to_high_low))
        rows_at = pl.ds(s * chunk, chunk)
        send(basis, basis_ref, rows_at, left_lanes)
        send(high, high_ref, rows_at, all_lanes)

    factor(second, upper, inverse, update, first_half)
    tri[HALF:, HALF:] = upper[...]
    send(tri, tri_ref, pl.ds(0, 2 * HALF), all_lanes)
    to_right = inverse_weights()
    chunk = rows // LAST
    for s in range(LAST):
        at = slice(s * chunk, (s + 1) * chunk)
        rh, rl = halves(rest[at])
        basis[at, HALF:] = fold(dot(jnp.concatenate([rh, rl], 1), to_right, ((1,), (1,))))
        send(basis, basis_ref, pl.ds(s * chunk, chunk), right_lanes)
    for copy in copies:
        copy.wait()


def sum_over_devices(packed, devices):
    if devices & (devices - 1) or devices < 32:
        return lax.psum(packed, AXES)

    def flip(value, masks):
        pairs = [(i, i ^ masks[i & 1]) for i in range(devices)]
        return lax.ppermute(value, AXES, pairs)

    def add_four(value, one, two):
        both = tuple(a ^ b for a, b in zip(one, two))
        first, second, third = flip(value, one), flip(value, two), flip(value, both)
        return (value + first) + (second + third)

    half = packed.shape[0] // 2
    mine = lax.axis_index(AXES) & 1
    parts = packed.reshape(2, half, packed.shape[1])
    total = lax.dynamic_index_in_dim(parts, mine, 0, False) + flip(
        lax.dynamic_index_in_dim(parts, 1 - mine, 0, False), (1, 1)
    )
    total = add_four(total, (2, 16), (8, 4))
    total = add_four(total, (16, 2), (4, 8))
    for bit in range(5, devices.bit_length() - 1):
        total = total + flip(total, (1 << bit, 1 << bit))
    other = flip(total, (1, 1))
    top = jnp.where(mine == 0, total, other)
    return jnp.concatenate([top, jnp.where(mine == 0, other, total)], 0)


def in_hbm(array):
    return pltpu.with_memory_space_constraint(array, pltpu.HBM)


def on_device(snapshots, live_rows, column_order, *, devices):
    rows, width = snapshots.shape
    smem = pl.BlockSpec(memory_space=pltpu.SMEM)
    vmem = pl.BlockSpec(memory_space=pltpu.VMEM)
    hbm = pl.BlockSpec(memory_space=pl.ANY)
    params = pltpu.CompilerParams(vmem_limit_bytes=VMEM_LIMIT)
    square = jax.ShapeDtypeStruct((width, width), jnp.float32)
    tall = jax.ShapeDtypeStruct((rows, width), jnp.float32)
    part = jax.ShapeDtypeStruct((rows, width), jnp.bfloat16)
    packed_rows = width + 2 * TILE
    packed, xh, xl = pl.pallas_call(
        functools.partial(gram_kernel, total_rows=rows * devices),
        in_specs=[smem, hbm, hbm],
        out_specs=[vmem, vmem, vmem],
        out_shape=[jax.ShapeDtypeStruct((packed_rows, HALF), jnp.float32), part, part],
        scratch_shapes=[
            pltpu.VMEM((rows, width), jnp.float32),
            pltpu.VMEM((1, width), jnp.int32),
            pltpu.SemaphoreType.DMA((LOADS + 1,)),
        ],
        compiler_params=params,
    )(live_rows, in_hbm(column_order.reshape(1, width)), in_hbm(snapshots))
    packed = sum_over_devices(packed, devices)
    block = pltpu.VMEM((HALF, HALF), jnp.float32)
    return pl.pallas_call(
        finish_kernel,
        in_specs=[vmem, vmem, vmem],
        out_specs=[hbm, hbm, hbm],
        out_shape=[tall, square, tall],
        scratch_shapes=[
            pltpu.VMEM((rows, width), jnp.float32),
            pltpu.VMEM((width, width), jnp.float32),
            pltpu.VMEM((rows, width), jnp.float32),
            pltpu.VMEM((rows, HALF), jnp.float32),
            block,
            block,
            block,
            pltpu.SemaphoreType.DMA((2 * PIECES + LAST + 1,)),
        ],
        compiler_params=params,
    )(packed, xh, xl)


def solution(mesh):
    placed = (P(AXES, None), P(AXES), P())
    return jax.shard_map(
        functools.partial(on_device, devices=mesh.size),
        mesh=mesh,
        in_specs=placed,
        out_specs=(P(AXES, None), P(), P(AXES, None)),
        check_vma=False,
    )
```

```python
import functools

import jax
import jax.numpy as jnp
from jax import lax
from jax.experimental import pallas as pl
from jax.experimental.pallas import tpu as pltpu
from jax.sharding import PartitionSpec as P

LOW = 32
HALF = 128
TILE = 8
WIDE = 2
AXES = ("lon", "lat", "depth")
VMEM_LIMIT = 16 * 1024 * 1024
LOADS = 1
PIECES = 8
LAST = 4


def dot(a, b, dims=((1,), (0,)), precision=None):
    return lax.dot_general(
        a, b, (dims, ((), ())), precision=precision, preferred_element_type=jnp.float32
    )


def halves(value):
    high = value.astype(jnp.bfloat16)
    return high, (value - high.astype(jnp.float32)).astype(jnp.bfloat16)


def one_hot(order_ref):
    count = order_ref.shape[1]
    source = lax.broadcasted_iota(jnp.int32, (count, count), 0)
    return jnp.where(source == order_ref[...], 1.0, 0.0).astype(jnp.bfloat16)


def square_iotas():
    return (
        lax.broadcasted_iota(jnp.int32, (HALF, HALF), 0),
        lax.broadcasted_iota(jnp.int32, (HALF, HALF), 1),
    )


def gram_kernel(
    live_ref, order_in, x_ref, packed_ref, high_ref, low_ref, held, order_ref, sems, *, total_rows
):
    rows, width = held.shape
    chunk = rows // LOADS
    fetch_order = pltpu.make_async_copy(order_in, order_ref, sems.at[LOADS])
    fetch_order.start()
    copies = []
    for c in range(LOADS):
        at = pl.ds(c * chunk, chunk)
        copies.append(pltpu.make_async_copy(x_ref.at[at], held.at[at], sems.at[c]))
        copies[-1].start()
    fetch_order.wait()
    pick = one_hot(order_ref)
    both = jnp.zeros((width, width), jnp.float32)
    cross = jnp.zeros((width, width), jnp.float32)
    down = ((0,), (0,))
    for c in range(LOADS):
        at = slice(c * chunk, (c + 1) * chunk)
        copies[c].wait()
        row = lax.broadcasted_iota(jnp.int32, (chunk, width), 0) + c * chunk
        high, low = halves(jnp.where(row < live_ref[0], held[at], 0.0))
        high = dot(high, pick).astype(jnp.bfloat16)
        low = dot(low, pick).astype(jnp.bfloat16)
        high_ref[at] = high
        low_ref[at] = low
        both = both + (dot(high, high, down) + dot(low, low, down))
        cross = cross + dot(high, low, down)
    gram = (both + (cross + cross.T)) / total_rows
    i, j = square_iotas()
    packed_ref[:HALF] = gram[:HALF, HALF:]
    last = gram[HALF:, HALF:]
    packed_ref[HALF : 2 * HALF] = jnp.where(i <= j, gram[:HALF, :HALF], last)
    packed_ref[2 * HALF :] = jnp.zeros((packed_ref.shape[0] - 2 * HALF, HALF), jnp.float32)
    packed_ref[2 * HALF : 2 * HALF + 1] = jnp.sum(jnp.where(i == j, last, 0.0), 0, keepdims=True)


def spread(value):
    return jnp.broadcast_to(value, (TILE, HALF))


def thirds(value):
    high = value.astype(jnp.bfloat16)
    rest = value - high.astype(jnp.float32)
    middle = rest.astype(jnp.bfloat16)
    return high, middle, (rest - middle.astype(jnp.float32)).astype(jnp.bfloat16)


def full_dot(a, b):
    ah, am, al = thirds(a)
    bh, bm, bl = thirds(b)
    pair = jnp.concatenate([bh, bm], 1)
    first = dot(jnp.concatenate([ah, am], 1), jnp.concatenate([pair, pair], 0))
    second = dot(jnp.concatenate([ah, al], 1), jnp.concatenate([bl, bh], 0))
    return first[:, :HALF] + (first[:, HALF:] + second)


def factor(matrix, upper_ref, inverse_ref, update_ref, beside):
    width = WIDE * TILE
    steps = HALF // width
    groups = HALF // TILE
    lanes = lax.broadcasted_iota(jnp.int32, (TILE, HALF), 1)
    subs = lax.broadcasted_iota(jnp.int32, (TILE, HALF), 0)
    rows = [matrix[g * TILE : (g + 1) * TILE] for g in range(groups)]
    update_ref[...] = jnp.zeros_like(update_ref)
    for s in range(steps):
        first = s * width
        mine = range(s * WIDE, (s + 1) * WIDE)
        near = range((s + 1) * WIDE, min((s + 2) * WIDE, groups))
        far = range((s + 2) * WIDE, groups)


        def pulled(g, q):
            only = jnp.where(lanes == first + q, rows[g], 0.0)
            return spread(jnp.sum(only, axis=1, keepdims=True))

        column = [[pulled(g, q) for g in mine] for q in range(width)]
        side = {g: [pulled(g, q) for q in range(width)] for g in near}
        panel = [rows[g] for g in mine]
        up, low, scale = [None] * WIDE, [None] * WIDE, [None] * WIDE
        for m in range(width):
            home, at = divmod(m, TILE)
            here = subs == at
            recip = 1.0 / spread(column[m][home][at : at + 1])
            times = list(column[m])
            times[home] = jnp.where(here, 0.0, times[home])
            times = [value * recip for value in times]
            for q in range(m + 1, width):
                value = spread(column[q][home][at : at + 1])
                column[q] = [c - t * value for c, t in zip(column[q], times)]
            lane = lanes == first + m
            up[home] = jnp.where(here, panel[home], up[home]) if at else panel[home]
            panel = [
                jnp.where(lane, jnp.where(here, 1.0, 0.0) if h == home else 0.0, panel[h])
                for h in range(WIDE)
            ]
            low[home] = jnp.where(here, panel[home], low[home]) if at else panel[home]
            scale[home] = jnp.where(here, recip, scale[home]) if at else recip
            row = spread(panel[home][at : at + 1])
            panel = [p - t * row for p, t in zip(panel, times)]
        for h, g in enumerate(mine):
            at = slice(g * TILE, (g + 1) * TILE)
            root = scale[h] * lax.rsqrt(scale[h])
            upper_ref[at] = jnp.where(lanes >= subs + g * TILE, up[h] * root, 0.0)
            inverse_ref[at] = jnp.where(lanes <= subs + g * TILE, low[h] * root, 0.0)
        inside = (lanes >= first) & (lanes < first + width)
        solved = [p * c for p, c in zip(panel, scale)]
        for g in near:
            terms = [
                side[g][h * TILE + i] * spread(solved[h][i : i + 1])
                for h in range(WIDE)
                for i in range(TILE)
            ]
            while len(terms) > 1:
                terms = [a + b for a, b in zip(terms[::2], terms[1::2])]
            rows[g] = jnp.where(inside, 0.0, rows[g]) - terms[0]
        if far:
            for h, g in enumerate(mine):
                update_ref[g * TILE : (g + 1) * TILE] = solved[h]
            if s:
                update_ref[first - width : first] = jnp.zeros((width, HALF), jnp.float32)
            change = full_dot(jnp.concatenate([rows[g] for g in far], 0), update_ref[...])
            for k, g in enumerate(far):
                rows[g] = jnp.where(inside, 0.0, rows[g]) - change[k * TILE : (k + 1) * TILE]
        beside(s)


def finish_kernel(
    packed_ref, xh_ref, xl_ref, basis_ref, tri_ref, high_ref,
    basis, tri, high, rest, upper, inverse, update, sems,
):
    rows = xh_ref.shape[0]
    chunk = rows // PIECES
    i, j = square_iotas()
    mixed = packed_ref[HALF : 2 * HALF]
    flipped = mixed.T
    first = jnp.where(i <= j, mixed, flipped)
    last = jnp.where(i > j, mixed, flipped)
    last = jnp.where(
        i == j, jnp.broadcast_to(packed_ref[2 * HALF : 2 * HALF + 1], (HALF, HALF)), last
    )
    side = packed_ref[:HALF]

    copies = []

    def send(source, target, at, lanes):
        copies.append(
            pltpu.make_async_copy(
                source.at[at, lanes], target.at[at, lanes], sems.at[len(copies)]
            )
        )
        copies[-1].start()

    def fold(value):
        return value[:, :HALF] + value[:, HALF:]

    left_lanes, right_lanes, all_lanes = pl.ds(0, HALF), pl.ds(HALF, HALF), pl.ds(0, 2 * HALF)
    factor(first, upper, inverse, update, lambda s: None)
    corner = full_dot(inverse[...], side)
    missed = side - full_dot(upper[...].T, corner)
    ih, im, _ = thirds(inverse[...])
    mh, mm, _ = thirds(missed)
    pair = jnp.concatenate([mh, mm], 1)
    corner = corner + fold(
        dot(jnp.concatenate([ih, im], 1), jnp.concatenate([pair, pair], 0))
    )
    tri[:HALF, :HALF] = upper[...]
    tri[:HALF, HALF:] = corner
    tri[HALF:, :HALF] = jnp.zeros((HALF, HALF), jnp.float32)
    second = last - full_dot(corner.T, corner)

    none = jnp.zeros((HALF, HALF), jnp.bfloat16)

    def inverse_weights():
        h, l = halves(inverse[...])
        return jnp.concatenate([jnp.concatenate([h, h], 1), jnp.concatenate([l, none], 1)], 0)

    to_left = inverse_weights()
    ch, cl = halves(corner)
    to_rest = jnp.concatenate([jnp.concatenate([ch, cl], 1), jnp.concatenate([ch, none], 1)], 0)
    th, tl = halves(tri[:LOW, :])
    blank = jnp.zeros((HALF - LOW, 2 * HALF), jnp.bfloat16)
    to_high = jnp.concatenate([th, blank, th, blank], 0)
    to_high_low = jnp.concatenate([tl, blank], 0)

    def first_half(s):
        at = slice(s * chunk, (s + 1) * chunk)
        xh, xl = xh_ref[at], xl_ref[at]
        left = fold(dot(jnp.concatenate([xh[:, :HALF], xl[:, :HALF]], 1), to_left, ((1,), (1,))))
        x = xh.astype(jnp.float32) + xl.astype(jnp.float32)
        basis[at, :HALF] = left
        lh, ll = halves(left)
        both = jnp.concatenate([lh, ll], 1)
        rest[at] = x[:, HALF:] - fold(dot(both, to_rest))
        high[at] = x - (dot(both, to_high) + dot(lh, to_high_low))
        rows_at = pl.ds(s * chunk, chunk)
        send(basis, basis_ref, rows_at, left_lanes)
        send(high, high_ref, rows_at, all_lanes)

    factor(second, upper, inverse, update, first_half)
    tri[HALF:, HALF:] = upper[...]
    send(tri, tri_ref, pl.ds(0, 2 * HALF), all_lanes)
    to_right = inverse_weights()
    chunk = rows // LAST
    for s in range(LAST):
        at = slice(s * chunk, (s + 1) * chunk)
        rh, rl = halves(rest[at])
        basis[at, HALF:] = fold(dot(jnp.concatenate([rh, rl], 1), to_right, ((1,), (1,))))
        send(basis, basis_ref, pl.ds(s * chunk, chunk), right_lanes)
    for copy in copies:
        copy.wait()


def sum_over_devices(packed, devices):
    if devices & (devices - 1) or devices < 32:
        return lax.psum(packed, AXES)

    def flip(value, masks):
        pairs = [(i, i ^ masks[i & 1]) for i in range(devices)]
        return lax.ppermute(value, AXES, pairs)

    def add_four(value, one, two):
        both = tuple(a ^ b for a, b in zip(one, two))
        first, second, third = flip(value, one), flip(value, two), flip(value, both)
        return (value + first) + (second + third)

    half = packed.shape[0] // 2
    mine = lax.axis_index(AXES) & 1
    parts = packed.reshape(2, half, packed.shape[1])
    total = lax.dynamic_index_in_dim(parts, mine, 0, False) + flip(
        lax.dynamic_index_in_dim(parts, 1 - mine, 0, False), (1, 1)
    )
    total = add_four(total, (2, 16), (8, 4))
    total = add_four(total, (16, 2), (4, 8))
    for bit in range(5, devices.bit_length() - 1):
        total = total + flip(total, (1 << bit, 1 << bit))
    other = flip(total, (1, 1))
    top = jnp.where(mine == 0, total, other)
    return jnp.concatenate([top, jnp.where(mine == 0, other, total)], 0)


def in_hbm(array):
    return pltpu.with_memory_space_constraint(array, pltpu.HBM)


def on_device(snapshots, live_rows, column_order, *, devices):
    rows, width = snapshots.shape
    smem = pl.BlockSpec(memory_space=pltpu.SMEM)
    vmem = pl.BlockSpec(memory_space=pltpu.VMEM)
    hbm = pl.BlockSpec(memory_space=pl.ANY)
    params = pltpu.CompilerParams(vmem_limit_bytes=VMEM_LIMIT)
    square = jax.ShapeDtypeStruct((width, width), jnp.float32)
    tall = jax.ShapeDtypeStruct((rows, width), jnp.float32)
    part = jax.ShapeDtypeStruct((rows, width), jnp.bfloat16)
    packed_rows = width + 2 * TILE
    packed, xh, xl = pl.pallas_call(
        functools.partial(gram_kernel, total_rows=rows * devices),
        in_specs=[smem, hbm, hbm],
        out_specs=[vmem, vmem, vmem],
        out_shape=[jax.ShapeDtypeStruct((packed_rows, HALF), jnp.float32), part, part],
        scratch_shapes=[
            pltpu.VMEM((rows, width), jnp.float32),
            pltpu.VMEM((1, width), jnp.int32),
            pltpu.SemaphoreType.DMA((LOADS + 1,)),
        ],
        compiler_params=params,
    )(live_rows, in_hbm(column_order.reshape(1, width)), in_hbm(snapshots))
    packed = sum_over_devices(packed, devices)
    block = pltpu.VMEM((HALF, HALF), jnp.float32)
    return pl.pallas_call(
        finish_kernel,
        in_specs=[vmem, vmem, vmem],
        out_specs=[hbm, hbm, hbm],
        out_shape=[tall, square, tall],
        scratch_shapes=[
            pltpu.VMEM((rows, width), jnp.float32),
            pltpu.VMEM((width, width), jnp.float32),
            pltpu.VMEM((rows, width), jnp.float32),
            pltpu.VMEM((rows, HALF), jnp.float32),
            block,
            block,
            block,
            pltpu.SemaphoreType.DMA((2 * PIECES + LAST + 1,)),
        ],
        compiler_params=params,
    )(packed, xh, xl)


def solution(mesh):
    placed = (P(AXES, None), P(AXES), P())
    return jax.shard_map(
        functools.partial(on_device, devices=mesh.size),
        mesh=mesh,
        in_specs=placed,
        out_specs=(P(AXES, None), P(), P(AXES, None)),
        check_vma=False,
    )
```
